32 devices in a mesh: prow: 4 (over y, x), pcol: 8 (over z, core).
Axes of the slice: x: 2, y: 2, z: 4, core: 2. Of those that a mesh axis runs over, the one named last changes fastest.
Arguments:
- ancestor_inverse: bfloat16 [6144, 6144], P('pcol', 'prow'), may hold values from -6 to 6
- lower_panel: bfloat16 [6144, 1024], P(('prow', 'pcol')), may hold values from -0.3125 to 0.3125
- pivot_inverse: float32 [256, 1024], P('pcol', 'prow'), may hold values from -6 to 6
- struct_list: int32 [4, 12], replicated, may hold values from -1 to 23, as said below
Outputs:
- off_inverse: bfloat16 [6144, 1024], P('pcol', 'prow')
- diag_inverse: float32 [256, 1024], P('pcol', 'prow')
The draws below stay inside these ranges and needn't reach their ends.
Inputs may be any that keep to these rules, and one draw needn't show every extreme that they name: `struct_list`: each row lists distinct ancestor supernodes first, all within 12 cyclically consecutive ancestor numbers, then entries -1; every row has at least one ancestor and some row lists 12.
All inputs are finite; a program needn't handle non-finite values.
Results may differ from the reference program's by a relative error of at most 0.001.
Values may be sent and summed in bfloat16 or wider, within the bound.
No kernel may reach another device: no remote copies, remote signals or barrier semaphores. Data moves between devices by JAX's collectives and lax.ppermute only.
A program may use at most 64 MiB of HBM per device.

```python
import jax
import jax.numpy as jnp
from jax import lax

B = 256
NK = 4
NA = 24
SLOTS = 12
GROUP = 6


def draw_struct_list(key, part):
    key_start, key_kept = jax.random.split(jax.random.fold_in(key, 11))
    window_start = jax.random.randint(key_start, (NK, 1), 0, NA)
    retained = jax.random.randint(key_kept, (NK, SLOTS), 0, 4) > 0
    offsets = jnp.arange(SLOTS, dtype=jnp.int32)[None, :]
    row_ids = jnp.arange(NK, dtype=jnp.int32)[:, None]
    retained = retained | (offsets == 0) | (row_ids == 0)
    ancestor_ids = (window_start + offsets) % NA
    sort_key = jnp.where(retained, offsets, offsets + SLOTS)
    ranking = jnp.argsort(sort_key, axis=1, stable=True)
    ids_sorted = jnp.take_along_axis(ancestor_ids, ranking, 1)
    kept_sorted = jnp.take_along_axis(retained, ranking, 1)
    return jnp.where(kept_sorted, ids_sorted, -1).astype(jnp.int32)


def with_spikes(drawn, own_key, source, target, parts, factor):
    def block_of(axis_at):
        return (jnp.arange(drawn.shape[axis_at]) // (drawn.shape[axis_at] // parts)).reshape((-1,) + (1,) * (drawn.ndim - 1 - axis_at))

    near = jax.random.permutation(own_key, parts)[block_of(target)]
    second = (block_of(target) + parts // 2) % parts
    return jnp.where((block_of(source) == near) | (block_of(source) == second), factor * drawn, drawn)


def block_scale(stream_key, shape, cuts, low, high):
    def one(position, shards_of):
        draws = jax.random.uniform(jax.random.fold_in(jax.random.fold_in(stream_key, 6), position), (shards_of,), jnp.float32, low / len(cuts), high / len(cuts))
        return jnp.repeat(jnp.exp(draws), shape[position] // shards_of).reshape((-1,) + (1,) * (len(shape) - position - 1))

    factor_of = one(*cuts[0])
    for cut in cuts[1:]:
        factor_of = factor_of * one(*cut)
    return factor_of


def centred(key, dims, deviation, limit, pieces=(), kind=jnp.bfloat16):
    loudness = block_scale(key, dims, pieces, -0.22, 0.18) if pieces else 1.0
    values = jax.random.normal(key, dims, jnp.float32) * deviation * loudness
    return jnp.minimum(jnp.maximum(values, -limit), limit).astype(kind)


def gaussian_with(key, dims, scale, limit, cuts, heavy, kind=jnp.bfloat16):
    entries = scale * jax.random.normal(key, dims, jnp.float32)
    if cuts:
        entries = entries * block_scale(key, dims, cuts, -0.22, 0.18)
    return jnp.clip(with_spikes(entries, jax.random.fold_in(key, 3), *heavy), -limit, limit).astype(kind)


def setup_inputs(seed: int = 0) -> dict:
    key_list = jax.random.split(jax.random.key(seed), 5)
    ancestor_inverse = centred(key_list[0], (NA * B, NA * B), 1.0, 6.0, ((0, 8), (1, 4)))
    lower_panel = gaussian_with(key_list[1], (NA * B, NK * B), (NA * B // 4) ** -0.5, 0.3125, ((0, 32),), (0, 1, 32, 2.75))
    pivot_inverse = centred(key_list[2], (B, NK * B), 1.0, 6.0, ((0, 8), (1, 4)), jnp.float32)
    struct_list = draw_struct_list(jax.random.fold_in(key_list[4], 71), 0)
    return {"ancestor_inverse": ancestor_inverse, "lower_panel": lower_panel, "pivot_inverse": pivot_inverse, "struct_list": struct_list}


def block_mask_of(struct_list):
    ancestors = jnp.arange(NA, dtype=jnp.int32)
    listed = struct_list[:, :, None] == ancestors[None, None, :]
    member = jnp.transpose(jnp.any(listed, axis=1)).astype(jnp.float32)
    return jnp.repeat(jnp.repeat(member, B, axis=0), B, axis=1)


def reference(ancestor_inverse, lower_panel, pivot_inverse, struct_list):
    block_mask = block_mask_of(struct_list)
    masked_lower = (lower_panel.astype(jnp.float32) * block_mask).astype(jnp.bfloat16)
    width = GROUP * B

    def add_group(group, total):
        columns = lax.dynamic_slice_in_dim(ancestor_inverse, group * width, width, 1)
        rows_part = lax.dynamic_slice_in_dim(masked_lower, group * width, width, 0)
        product = -jnp.dot(columns, rows_part, preferred_element_type=jnp.float32)
        return total + product

    summed = lax.fori_loop(0, NA // GROUP, add_group, jnp.zeros((NA * B, NK * B), jnp.float32))
    off_sum = summed * block_mask
    off_inverse = off_sum.astype(jnp.bfloat16)
    lower_blocks = masked_lower.astype(jnp.float32).reshape(NA * B, NK, B)
    off_blocks = off_sum.reshape(NA * B, NK, B)
    diag_term = jnp.einsum("ikr,ikc->rkc", lower_blocks, off_blocks, precision=lax.Precision.HIGHEST).reshape(B, NK * B)
    diag_inverse = pivot_inverse - diag_term
    return off_inverse, diag_inverse
```

```python
import functools

import jax
import jax.numpy as jnp
from jax import lax
from jax.experimental import pallas as pl
from jax.experimental.pallas import tpu as pltpu
from jax.sharding import PartitionSpec as P

B = 256
NK = 4
AXES = ("prow", "pcol")
HALF = 128
TAIL = 16


def from_root(value, axis, root):
    mine = lax.axis_index(axis) == root
    return lax.psum(jnp.where(mine, value, jnp.zeros_like(value)), axis)


def membership(struct_list, ancestor_ids):
    listed = struct_list[:, :, None] == ancestor_ids[None, None, :]
    return jnp.transpose(jnp.any(listed, axis=1))


def general_body(ancestor_inverse, lower_panel, pivot_inverse, struct_list):
    row_count = ancestor_inverse.shape[0] // B
    col_count = ancestor_inverse.shape[1] // B
    grid_rows = lax.axis_size("prow")
    prow_index = lax.axis_index("prow")
    pcol_index = lax.axis_index("pcol")
    col_share = NK * B // grid_rows
    gathered = lax.all_gather(lower_panel, "pcol", axis=0, tiled=True)
    col_ids = prow_index * col_count + jnp.arange(col_count, dtype=jnp.int32)
    row_ids = pcol_index * row_count + jnp.arange(row_count, dtype=jnp.int32)
    member_cols = membership(struct_list, col_ids)
    member_rows = membership(struct_list, row_ids)
    scaled = gathered.reshape(col_count, B, NK, B) * member_cols[:, None, :, None].astype(
        jnp.bfloat16
    )
    masked = scaled.reshape(col_count * B, NK * B)
    partial_value = -jnp.dot(ancestor_inverse, masked, preferred_element_type=jnp.float32)
    share_sum = lax.psum_scatter(partial_value, "prow", scatter_dimension=1, tiled=True)
    columns = prow_index * col_share + jnp.arange(col_share, dtype=jnp.int32)
    block_of = columns // B
    one_hot = block_of[:, None] == jnp.arange(NK, dtype=jnp.int32)[None, :]
    row_mask = jnp.any(member_rows[:, None, :] & one_hot[None, :, :], axis=2).astype(jnp.float32)
    off_share = (share_sum.reshape(row_count, B, col_share) * row_mask[:, None, :]).reshape(
        row_count * B, col_share
    )
    off_inverse = off_share.astype(jnp.bfloat16)
    block_count = max(col_share // B, 1)
    column_width = col_share // block_count
    offset_blocks = pcol_index * row_count % col_count
    root_row = pcol_index * row_count // col_count
    piece = lax.dynamic_slice_in_dim(masked, offset_blocks * B, row_count * B, 0)
    lower_rows = from_root(piece, "prow", root_row)
    first_block = prow_index * col_share // B
    lower_slice = lax.dynamic_slice_in_dim(lower_rows, first_block * B, block_count * B, 1)
    lower_blocks = lower_slice.astype(jnp.float32).reshape(row_count * B, block_count, B)
    off_blocks = off_share.reshape(row_count * B, block_count, column_width)
    diag_term = jnp.einsum(
        "ikr,ikc->rkc", lower_blocks, off_blocks, precision=lax.Precision.HIGHEST
    ).reshape(B, col_share)
    diag_share = lax.psum_scatter(diag_term, "pcol", scatter_dimension=0, tiled=True)
    diag_inverse = pivot_inverse - diag_share
    return (off_inverse, diag_inverse)


ANY = pl.BlockSpec(memory_space=pl.ANY)
VM = pl.BlockSpec(memory_space=pltpu.VMEM)
SM = pl.BlockSpec(memory_space=pltpu.SMEM)


def place():
    p = lax.axis_index("prow")
    q = lax.axis_index("pcol")
    return p, q // 2, q % 2


def is_member(struct_ref, level, ancestor):
    found = struct_ref[level, 0] == ancestor
    for slot in range(1, struct_ref.shape[1]):
        found = found | (struct_ref[level, slot] == ancestor)
    return found


def call(kernel, outs, specs, scratch, flops, moved, name):
    return pl.pallas_call(
        kernel,
        out_shape=outs,
        in_specs=specs,
        out_specs=jax.tree.map(lambda _: VM, outs),
        scratch_shapes=scratch,
        compiler_params=pltpu.CompilerParams(vmem_limit_bytes=40 * 2**20),
        cost_estimate=pl.CostEstimate(flops=flops, bytes_accessed=moved, transcendentals=0),
        name=name,
    )


def split_kernel(struct_ref, lower_ref, across_ref, first_ref, second_ref, own_ref):
    p, z, c = place()
    shard = lower_ref.shape[0]
    start = (p * 8 + 2 * z + c) * shard
    ancestor = start // B
    edge = (ancestor + 1) * B - start
    row = lax.broadcasted_iota(jnp.int32, (shard, B), 0)

    def masked(flip):
        level = p ^ flip
        value = lower_ref[:, pl.ds(pl.multiple_of(level * B, B), B)]
        low = is_member(struct_ref, level, ancestor).astype(jnp.int32)
        high = is_member(struct_ref, level, ancestor + 1).astype(jnp.int32)
        keep = jnp.where(row < edge, low, high) > 0
        return jnp.where(keep, value.astype(jnp.float32), 0.0).astype(jnp.bfloat16)

    across_ref[...] = masked(3)
    x_part = masked(1)
    y_part = masked(2)
    first_ref[:shard] = x_part[:, :HALF]
    first_ref[shard:] = y_part[:, :HALF]
    second_ref[:shard] = x_part[:, HALF:]
    second_ref[shard:] = y_part[:, HALF:]
    own_ref[...] = masked(0)


def assemble(pieces, panel, sems, shard, halves):
    _, z, c = place()
    middle = (z == 1) | (z == 2)

    def copies(ref, flip, core, index):
        at = pl.multiple_of(((z ^ flip) * 2 + core) * shard, shard)
        if halves:
            return [
                pltpu.make_async_copy(
                    ref.at[pl.ds(h * shard, shard)],
                    panel.at[pl.ds(at, shard), pl.ds(h * HALF, HALF)],
                    sems.at[index, h],
                )
                for h in range(2)
            ]
        return [pltpu.make_async_copy(ref, panel.at[pl.ds(at, shard)], sems.at[index, 0])]

    plan = []
    for side in range(2):
        core = c if side == 0 else 1 - c
        for slot, flip in enumerate((0, 1, 2, 3, 3)):
            cond = None if slot < 3 else (middle if slot == 3 else jnp.logical_not(middle))
            plan.append((cond, copies(pieces[side * 5 + slot], flip, core, side * 5 + slot)))

    def each(act):
        for cond, items in plan:
            def go(items=items):
                for item in items:
                    act(item)
            if cond is None:
                go()
            else:
                pl.when(cond)(go)

    each(lambda item: item.start())
    return lambda: each(lambda item: item.wait())


def encode(value):
    top = jnp.max(jnp.abs(value), axis=0, keepdims=True)
    power = jnp.floor(jnp.log2(jnp.maximum(top, 2e-34))) + 1.0
    scaled = jnp.round(value * jnp.exp2(15.0 - power))
    code = jnp.clip(scaled, -32767.0, 32767.0).astype(jnp.int32).astype(jnp.int16)
    return code, power


def put_coded(ref, values, block):
    code, power = encode(values)
    ref[block * B : (block + 1) * B] = code
    return power


def put_tail(ref, powers):
    rows = len(powers) * B
    row = lax.broadcasted_iota(jnp.int32, (TAIL, HALF), 0)
    tail = jnp.zeros((TAIL, HALF), jnp.float32)
    for block, power in enumerate(powers):
        tail = jnp.where(row == block, power, tail)
    ref[rows : rows + TAIL] = tail.astype(jnp.int32).astype(jnp.int16)


def decode(ref, block, blocks):
    tail = ref[blocks * B : blocks * B + TAIL].astype(jnp.int32).astype(jnp.float32)
    step = jnp.exp2(tail[block : block + 1] - 15.0)
    code = ref[block * B : (block + 1) * B].astype(jnp.int32).astype(jnp.float32)
    return code * step


def start_rows(a_ref, a_buf, sems):
    blocks = a_buf.shape[0] // B
    items = [
        pltpu.make_async_copy(a_ref.at[pl.ds(b * B, B)], a_buf.at[pl.ds(b * B, B)], sems.at[b])
        for b in range(blocks)
    ]
    for item in items:
        item.start()
    return items


def chunk_kernel(kind, shard, *refs):
    pieces = refs[:10]
    a_ref = refs[10]
    at = 11
    came = None
    if kind != "across":
        came = refs[11]
        at = 12
    left_ref, right_ref = refs[at : at + 2]
    lower_refs = refs[at + 2 : len(refs) - 4]
    panel, a_buf, piece_sems, row_sems = refs[len(refs) - 4 :]
    _, _, c = place()
    halves = kind != "across"
    wait_pieces = assemble(pieces, panel, piece_sems, shard, halves)
    rows = start_rows(a_ref, a_buf, row_sems)
    wait_pieces()
    blocks = len(rows)
    left_powers, right_powers = [], []
    for b in range(blocks):
        rows[b].wait()
        total = -jnp.dot(
            a_buf[b * B : (b + 1) * B], panel[...], preferred_element_type=jnp.float32
        )
        left, right = total[:, :HALF], total[:, HALF:]
        if kind == "first":
            right = right + decode(came, b, blocks)
        if kind == "second":
            left = left + decode(came, b, blocks)
        left_powers.append(put_coded(left_ref, left, b))
        right_powers.append(put_coded(right_ref, right, b))
    put_tail(left_ref, left_powers)
    put_tail(right_ref, right_powers)
    share = blocks * B
    kept = panel[pl.ds(pl.multiple_of(c * share, share), share)]
    if halves:
        lower_refs[0][...] = kept[:, :HALF]
        lower_refs[1][...] = kept[:, HALF:]
    else:
        lower_refs[0][...] = kept


def last_kernel(shard, *refs):
    pieces = refs[:10]
    a_ref, struct_ref, xa, ya, xb, yb, l_across, l_xa, l_ya, l_xb, l_yb = refs[10:21]
    off_ref, diag_ref = refs[21:23]
    panel, a_buf, lower, piece_sems, row_sems, lower_sems = refs[23:]
    p, z, c = place()
    wait_pieces = assemble(pieces, panel, piece_sems, shard, False)
    rows = start_rows(a_ref, a_buf, row_sems)
    share = lower.shape[0]
    flip = p ^ z

    def lower_copies(flip):
        if flip == 3:
            return [pltpu.make_async_copy(l_across, lower, lower_sems.at[0])]
        pair = (l_xa, l_xb) if flip == 1 else (l_ya, l_yb)
        return [
            pltpu.make_async_copy(pair[h], lower.at[:, pl.ds(h * HALF, HALF)], lower_sems.at[h])
            for h in range(2)
        ]

    for known in (1, 2, 3):
        @pl.when(flip == known)
        def _(known=known):
            for item in lower_copies(known):
                item.start()

    wait_pieces()

    @pl.when(flip == 0)
    def _():
        lower[...] = panel[pl.ds(pl.multiple_of(c * share, share), share)]

    for known in (1, 2, 3):
        @pl.when(flip == known)
        def _(known=known):
            for item in lower_copies(known):
                item.wait()

    blocks = len(rows)
    first = (2 * z + c) * blocks
    diag = jnp.zeros((B, B), jnp.float32)
    contract = (((0,), (0,)), ((), ()))
    for b in range(blocks):
        rows[b].wait()
        total = -jnp.dot(
            a_buf[b * B : (b + 1) * B], panel[...], preferred_element_type=jnp.float32
        )
        left = total[:, :HALF] + (decode(xa, b, blocks) + decode(ya, b, blocks))
        right = total[:, HALF:] + (decode(xb, b, blocks) + decode(yb, b, blocks))
        total = jnp.concatenate([left, right], axis=1)
        keep = is_member(struct_ref, p, first + b).astype(jnp.float32)
        total = total * keep
        high = total.astype(jnp.bfloat16)
        low = (total - high.astype(jnp.float32)).astype(jnp.bfloat16)
        off_ref[b * B : (b + 1) * B] = high
        factor = lower[b * B : (b + 1) * B]
        for part in (high, low):
            diag = diag + lax.dot_general(
                factor, part, contract, preferred_element_type=jnp.float32
            )
    piece = B // 8
    panel_diag = diag_ref
    for place_of in range(8):
        panel_diag[pl.ds(pl.multiple_of((place_of ^ (2 * z + c)) * piece, piece), piece)] = diag[
            place_of * piece : (place_of + 1) * piece
        ]


def pairs(move):
    found = []
    for p in range(4):
        for z in range(4):
            for c in range(2):
                to = move(p, z, c)
                if to is not None:
                    found.append((p * 8 + 2 * z + c, to[0] * 8 + 2 * to[1] + to[2]))
    return found


def send(value, move):
    return lax.ppermute(value, AXES, pairs(move))


def mids(z):
    return z in (1, 2)


def gather(own):
    one = send(own, lambda p, z, c: (p, z ^ 1, c))
    two = send(own, lambda p, z, c: (p, z ^ 2, c))
    mid = send(own, lambda p, z, c: (p, z ^ 3, c) if mids(z) else None)
    end = send(two, lambda p, z, c: (p, z ^ 1, c) if mids(z) else None)
    kept = [own, one, two, mid, end]
    swap = lambda p, z, c: (p, z, 1 - c)
    others = [
        send(own, swap),
        send(one, swap),
        send(two, swap),
        send(mid, lambda p, z, c: (p, z, 1 - c) if mids(z) else None),
        send(end, lambda p, z, c: None if mids(z) else (p, z, 1 - c)),
    ]
    return kept + others


def to_flip(flip):
    return lambda p, z, c: (p ^ flip, z, c)


def from_home(flip):
    return lambda p, z, c: (p ^ flip, z, c) if p == z else None


def line_body(ancestor_inverse, lower_panel, pivot_inverse, struct_list):
    rows, depth = ancestor_inverse.shape
    shard = lower_panel.shape[0]
    blocks = rows // B
    bf16, f32 = jnp.bfloat16, jnp.float32
    across, first, second, own = call(
        split_kernel,
        (
            jax.ShapeDtypeStruct((shard, B), bf16),
            jax.ShapeDtypeStruct((2 * shard, HALF), bf16),
            jax.ShapeDtypeStruct((2 * shard, HALF), bf16),
            jax.ShapeDtypeStruct((shard, B), bf16),
        ),
        [SM, VM],
        [],
        shard * NK * B,
        4 * shard * NK * B,
        "split_lower",
    )(struct_list, lower_panel)

    coded = jax.ShapeDtypeStruct((rows + TAIL, HALF), jnp.int16)
    scratch = [
        pltpu.VMEM((depth, B), bf16),
        pltpu.VMEM((rows, depth), bf16),
        pltpu.SemaphoreType.DMA((10, 2)),
        pltpu.SemaphoreType.DMA((blocks,)),
    ]
    flops = 2 * rows * depth * B
    moved = 2 * rows * depth

    def chunk(kind, pieces, came):
        if kind == "across":
            lower = (jax.ShapeDtypeStruct((rows, B), bf16),)
        else:
            lower = (jax.ShapeDtypeStruct((rows, HALF), bf16),) * 2
        extra = [] if came is None else [came]
        return call(
            functools.partial(chunk_kernel, kind, shard),
            (coded, coded) + lower,
            [ANY] * 11 + [VM] * len(extra),
            scratch,
            flops,
            moved,
            "chunk_" + kind,
        )(*pieces, ancestor_inverse, *extra)

    to_x, to_y, lower_a = chunk("across", gather(across), None)
    by_x = send(to_x, to_flip(1))
    by_y = send(to_y, to_flip(2))
    l_across = send(lower_a, from_home(3))

    xa, ya, l_xa, l_ya = chunk("first", gather(first), by_x)
    xa = send(xa, to_flip(1))
    ya = send(ya, to_flip(2))
    l_xa = send(l_xa, from_home(1))
    l_ya = send(l_ya, from_home(2))

    xb, yb, l_xb, l_yb = chunk("second", gather(second), by_y)
    xb = send(xb, to_flip(1))
    yb = send(yb, to_flip(2))
    l_xb = send(l_xb, from_home(1))
    l_yb = send(l_yb, from_home(2))

    off_inverse, diag = call(
        functools.partial(last_kernel, shard),
        (jax.ShapeDtypeStruct((rows, B), bf16), jax.ShapeDtypeStruct((B, B), f32)),
        [ANY] * 11 + [SM] + [VM] * 4 + [ANY] * 5,
        scratch[:2]
        + [pltpu.VMEM((rows, B), bf16)]
        + scratch[2:]
        + [pltpu.SemaphoreType.DMA((2,))],
        flops,
        moved,
        "chunk_own",
    )(*gather(own), ancestor_inverse, struct_list, xa, ya, xb, yb, l_across, l_xa, l_ya, l_xb, l_yb)

    piece = B // 8
    total = diag[:piece]
    for flip in range(1, 8):
        part = diag[flip * piece : (flip + 1) * piece]
        total = total + send(part, lambda p, z, c: (p, z ^ (flip >> 1), c ^ (flip & 1)))
    return off_inverse, pivot_inverse - total


def body(ancestor_inverse, lower_panel, pivot_inverse, struct_list):
    rows, depth = ancestor_inverse.shape
    shard = lower_panel.shape[0]
    line = (
        lax.axis_size("prow") == 4
        and lax.axis_size("pcol") == 8
        and depth == 8 * shard
        and depth == 2 * rows
        and shard % 64 == 0
        and shard <= B
    )
    plan = line_body if line else general_body
    return plan(ancestor_inverse, lower_panel, pivot_inverse, struct_list)


def solution(mesh):
    placed = (P("pcol", "prow"), P(("prow", "pcol"), None), P("pcol", "prow"), P())
    return jax.shard_map(
        body,
        mesh=mesh,
        in_specs=placed,
        out_specs=(P("pcol", "prow"), P("pcol", "prow")),
        check_vma=False,
    )
```

```python
import functools

import jax
import jax.numpy as jnp
from jax import lax
from jax.experimental import pallas as pl
from jax.experimental.pallas import tpu as pltpu
from jax.sharding import PartitionSpec as P

B = 256
NK = 4
AXES = ("prow", "pcol")
HALF = 128
TAIL = 16


def from_root(value, axis, root):
    mine = lax.axis_index(axis) == root
    return lax.psum(jnp.where(mine, value, jnp.zeros_like(value)), axis)


def membership(struct_list, ancestor_ids):
    listed = struct_list[:, :, None] == ancestor_ids[None, None, :]
    return jnp.transpose(jnp.any(listed, axis=1))


def general_body(ancestor_inverse, lower_panel, pivot_inverse, struct_list):
    row_count = ancestor_inverse.shape[0] // B
    col_count = ancestor_inverse.shape[1] // B
    grid_rows = lax.axis_size("prow")
    prow_index = lax.axis_index("prow")
    pcol_index = lax.axis_index("pcol")
    col_share = NK * B // grid_rows
    gathered = lax.all_gather(lower_panel, "pcol", axis=0, tiled=True)
    col_ids = prow_index * col_count + jnp.arange(col_count, dtype=jnp.int32)
    row_ids = pcol_index * row_count + jnp.arange(row_count, dtype=jnp.int32)
    member_cols = membership(struct_list, col_ids)
    member_rows = membership(struct_list, row_ids)
    scaled = gathered.reshape(col_count, B, NK, B) * member_cols[:, None, :, None].astype(
        jnp.bfloat16
    )
    masked = scaled.reshape(col_count * B, NK * B)
    partial_value = -jnp.dot(ancestor_inverse, masked, preferred_element_type=jnp.float32)
    share_sum = lax.psum_scatter(partial_value, "prow", scatter_dimension=1, tiled=True)
    columns = prow_index * col_share + jnp.arange(col_share, dtype=jnp.int32)
    block_of = columns // B
    one_hot = block_of[:, None] == jnp.arange(NK, dtype=jnp.int32)[None, :]
    row_mask = jnp.any(member_rows[:, None, :] & one_hot[None, :, :], axis=2).astype(jnp.float32)
    off_share = (share_sum.reshape(row_count, B, col_share) * row_mask[:, None, :]).reshape(
        row_count * B, col_share
    )
    off_inverse = off_share.astype(jnp.bfloat16)
    block_count = max(col_share // B, 1)
    column_width = col_share // block_count
    offset_blocks = pcol_index * row_count % col_count
    root_row = pcol_index * row_count // col_count
    piece = lax.dynamic_slice_in_dim(masked, offset_blocks * B, row_count * B, 0)
    lower_rows = from_root(piece, "prow", root_row)
    first_block = prow_index * col_share // B
    lower_slice = lax.dynamic_slice_in_dim(lower_rows, first_block * B, block_count * B, 1)
    lower_blocks = lower_slice.astype(jnp.float32).reshape(row_count * B, block_count, B)
    off_blocks = off_share.reshape(row_count * B, block_count, column_width)
    diag_term = jnp.einsum(
        "ikr,ikc->rkc", lower_blocks, off_blocks, precision=lax.Precision.HIGHEST
    ).reshape(B, col_share)
    diag_share = lax.psum_scatter(diag_term, "pcol", scatter_dimension=0, tiled=True)
    diag_inverse = pivot_inverse - diag_share
    return (off_inverse, diag_inverse)


VM = pl.BlockSpec(memory_space=pltpu.VMEM)
SM = pl.BlockSpec(memory_space=pltpu.SMEM)


def place():
    p = lax.axis_index("prow")
    q = lax.axis_index("pcol")
    return p, q // 2, q % 2


def call(kernel, outs, specs, scratch, flops, moved, name):
    return pl.pallas_call(
        kernel,
        out_shape=outs,
        in_specs=specs,
        out_specs=jax.tree.map(lambda _: VM, outs),
        scratch_shapes=scratch,
        compiler_params=pltpu.CompilerParams(vmem_limit_bytes=16 * 2**20),
        cost_estimate=pl.CostEstimate(flops=flops, bytes_accessed=moved, transcendentals=0),
        name=name,
    )


def split_kernel(lower_ref, near_ref, to_x, to_y, to_both, keep, sems):
    p, _, _ = place()
    shard = lower_ref.shape[0]
    moves = []

    def move(flip, start, width, out, slot, lane):
        at = pl.multiple_of((p ^ flip) * B + start, HALF)
        item = pltpu.make_async_copy(
            lower_ref.at[:, pl.ds(at, width)],
            out.at[pl.ds(slot * shard, shard), pl.ds(lane, width)],
            sems.at[len(moves)],
        )
        item.start()
        moves.append(item)

    move(3, 0, B, near_ref, 0, 0)
    move(1, 0, HALF, near_ref, 0, B)
    move(2, HALF, HALF, near_ref, 0, B + HALF)
    move(1, HALF, HALF, near_ref, 1, 0)
    move(2, 0, HALF, near_ref, 1, HALF)
    move(0, 0, B, near_ref, 1, B)
    for flip, out in ((1, to_x), (2, to_y), (3, to_both), (0, keep)):
        move(flip, 0, B, out, 0, 0)
    for item in moves:
        item.wait()


def pair_kernel(own_ref, one_ref, out_ref):
    shard = own_ref.shape[0] // 2
    out_ref[:shard] = own_ref[shard:]
    out_ref[shard : 2 * shard] = one_ref[shard:]


def pack_kernel(*refs):
    out_ref = refs[-1]
    _, z, _ = place()
    shard = out_ref.shape[0] // 4
    parts = (
        ((refs[0], 0), (refs[0], 1), (refs[1], 0), (refs[1], 1))
        if len(refs) == 3
        else tuple((ref, 0) for ref in refs[:4])
    )
    for flip, (ref, slot) in enumerate(parts):
        out_ref[pl.ds(pl.multiple_of((z ^ flip) * shard, 64), shard)] = ref[
            slot * shard : (slot + 1) * shard
        ]


def assemble(mine, theirs, panel, table_ref, parts):
    p, _, c = place()
    shard = panel.shape[0] // 8
    for zz in range(4):
        for ref, core in ((mine, c), (theirs, 1 - c)):
            at = pl.multiple_of((2 * zz + core) * shard, 64)
            panel[pl.ds(at, shard)] = ref[zz * shard : (zz + 1) * shard]
    blocks = panel.shape[0] // B
    for block in range(blocks):
        for flip, lane, width in parts:
            listed = table_ref[p ^ flip, p * blocks + block]

            @pl.when(listed == 0)
            def _(block=block, lane=lane, width=width):
                panel[block * B : (block + 1) * B, lane : lane + width] = jnp.zeros(
                    (B, width), jnp.bfloat16
                )


def encode(value):
    top = jnp.max(jnp.abs(value), axis=0, keepdims=True)
    power = jnp.floor(jnp.log2(jnp.maximum(top, 2e-34))) + 1.0
    scaled = jnp.round(value * jnp.exp2(15.0 - power))
    code = jnp.clip(scaled, -32767.0, 32767.0).astype(jnp.int32).astype(jnp.int16)
    return code, power


def put_coded(ref, values, block, first=0):
    code, power = encode(values)
    ref[first + block * B : first + (block + 1) * B] = code
    return power


def put_tail(ref, powers, first=0):
    rows = first + len(powers) * B
    row = lax.broadcasted_iota(jnp.int32, (TAIL, HALF), 0)
    tail = jnp.zeros((TAIL, HALF), jnp.float32)
    for block, power in enumerate(powers):
        tail = jnp.where(row == block, power, tail)
    ref[rows : rows + TAIL] = tail.astype(jnp.int32).astype(jnp.int16)


def decode(ref, block, blocks, first=0):
    last = first + blocks * B
    tail = ref[last : last + TAIL].astype(jnp.int32).astype(jnp.float32)
    step = jnp.exp2(tail[block : block + 1] - 15.0)
    code = ref[first + block * B : first + (block + 1) * B]
    return code.astype(jnp.int32).astype(jnp.float32) * step


def first_kernel(table_ref, a_ref, mine, theirs, x_ref, y_ref, panel):
    assemble(mine, theirs, panel, table_ref, ((3, 0, B), (1, B, HALF), (2, B + HALF, HALF)))
    blocks = a_ref.shape[0] // B
    share = blocks * B + TAIL
    places = ((x_ref, 0), (y_ref, 0), (x_ref, share), (y_ref, share))
    powers = [[], [], [], []]
    for b in range(blocks):
        total = -jnp.dot(
            a_ref[b * B : (b + 1) * B], panel[...], preferred_element_type=jnp.float32
        )
        for i, (ref, first) in enumerate(places):
            part = total[:, i * HALF : (i + 1) * HALF]
            powers[i].append(put_coded(ref, part, b, first))
    for (ref, first), power in zip(places, powers):
        put_tail(ref, power, first)


def second_kernel(
    table_ref, a_ref, mine, theirs, by_x, by_y, x_ref, y_ref, own_ref, panel
):
    assemble(mine, theirs, panel, table_ref, ((1, 0, HALF), (2, HALF, HALF), (0, B, B)))
    blocks = a_ref.shape[0] // B
    x_powers, y_powers = [], []
    for b in range(blocks):
        rows = slice(b * B, (b + 1) * B)
        total = -jnp.dot(a_ref[rows], panel[...], preferred_element_type=jnp.float32)
        x_powers.append(put_coded(x_ref, total[:, :HALF] + decode(by_y, b, blocks), b))
        y_powers.append(put_coded(y_ref, total[:, HALF:B] + decode(by_x, b, blocks), b))
        own_ref[rows] = total[:, B:]
    put_tail(x_ref, x_powers)
    put_tail(y_ref, y_powers)


def sum_kernel(table_ref, own_ref, x_first, y_first, x_second, y_second, off_ref, rest_ref):
    p, z, c = place()
    blocks = off_ref.shape[0] // B
    share = blocks * B + TAIL
    first = (2 * z + c) * blocks
    for b in range(blocks):
        rows = slice(b * B, (b + 1) * B)
        left = decode(x_first, b, blocks, share) + decode(y_second, b, blocks)
        right = decode(y_first, b, blocks, share) + decode(x_second, b, blocks)
        total = own_ref[rows] + jnp.concatenate([left, right], axis=1)
        total = jnp.where(table_ref[p, first + b] > 0, total, 0.0)
        high = total.astype(jnp.bfloat16)
        off_ref[rows] = high
        rest_ref[rows] = (total - high.astype(jnp.float32)).astype(jnp.bfloat16)


def route_kernel(own, x, y, both, *outs):
    p, z, _ = place()
    for flip, out in enumerate(outs):
        for turn, ref in enumerate((own, x, y, both)):

            @pl.when((p ^ z) == (turn ^ flip))
            def _(ref=ref, out=out):
                out[...] = ref[...]


def share_kernel(own, one, two, three, keep_ref, give_ref):
    _, z, c = place()
    shard = own.shape[0]
    for flip, ref in enumerate((own, one, two, three)):
        chip = z ^ flip
        at = pl.multiple_of((chip % 2) * shard, 64)

        @pl.when(chip // 2 == c)
        def _(ref=ref, at=at):
            keep_ref[pl.ds(at, shard)] = ref[...]

        @pl.when(chip // 2 != c)
        def _(ref=ref, at=at):
            give_ref[pl.ds(at, shard)] = ref[...]


def diag_kernel(off_ref, rest_ref, keep, came, diag_ref, lower):
    _, z, c = place()
    shard = keep.shape[0] // 2
    for half in range(2):
        for ref, core in ((keep, c), (came, 1 - c)):
            at = pl.multiple_of((2 * half + core) * shard, 64)
            lower[pl.ds(at, shard)] = ref[half * shard : (half + 1) * shard]
    contract = (((0,), (0,)), ((), ()))
    diag = lax.dot_general(
        lower[...], off_ref[...], contract, preferred_element_type=jnp.float32
    ) + lax.dot_general(
        lower[...], rest_ref[...], contract, preferred_element_type=jnp.float32
    )
    piece = B // 8
    for zz in range(4):
        for cc in range(2):
            slot = (cc ^ c) * 4 + (zz ^ z)
            at = (2 * zz + cc) * piece
            diag_ref[pl.ds(pl.multiple_of(slot * piece, piece), piece)] = diag[at : at + piece]


def send(value, move):
    found = []
    for p in range(4):
        for z in range(4):
            for c in range(2):
                to = move(p, z, c)
                found.append((p * 8 + 2 * z + c, to[0] * 8 + 2 * to[1] + to[2]))
    return lax.ppermute(value, AXES, found)


def chip_swap(p, z, c):
    return (p, z, 1 - c)


def along(flip):
    return lambda p, z, c: (p, z ^ flip, c)


def across(flip):
    return lambda p, z, c: (p ^ flip, z, c)


def after(value, *earlier):
    return lax.optimization_barrier((value, *earlier))[0]


def line_body(ancestor_inverse, lower_panel, pivot_inverse, struct_list):
    rows, depth = ancestor_inverse.shape
    shard = lower_panel.shape[0]
    bf16, f32, i16 = jnp.bfloat16, jnp.float32, jnp.int16
    shape = jax.ShapeDtypeStruct
    wide = 2 * B
    moved = 2 * rows * depth
    flops = 2 * rows * depth * wide

    def small(kernel, outs, name, *args, specs=None, scratch=()):
        return call(
            kernel, outs, specs or [VM] * len(args), list(scratch), shard * B, shard * B, name
        )(*args)

    piece = shape((shard, B), bf16)
    near, to_x, to_y, to_both, keep = small(
        split_kernel,
        (shape((2 * shard, wide), bf16), piece, piece, piece, piece),
        "split_lower",
        lower_panel,
        specs=[pl.BlockSpec(memory_space=pl.ANY)],
        scratch=[pltpu.SemaphoreType.DMA((10,))],
    )
    names = jnp.arange(4 * depth // B, dtype=jnp.int32)
    table = jnp.any(struct_list[:, :, None] == names, axis=1).astype(jnp.int32)

    line = shape((4 * shard, wide), bf16)
    panel = [pltpu.VMEM((depth, wide), bf16)]
    coded = shape((rows + TAIL, HALF), i16)
    coded_two = shape((2 * (rows + TAIL), HALF), i16)

    own = near[:shard]
    one = send(near, along(1))
    two = send(own, along(2))
    three = send(own, along(3))
    rows_x = send(to_x, across(1))
    rows_y = send(to_y, across(2))
    rows_both = send(to_both, across(3))
    mine = small(
        pack_kernel, line, "pack_first", own, one[:shard], two, after(three, rows_x, rows_y, rows_both)
    )
    pair = small(pair_kernel, shape((2 * shard + TAIL, wide), bf16), "pair", near, one)
    stay, to_one, to_two, to_three = small(
        route_kernel, (piece,) * 4, "route", keep, rows_x, rows_y, rows_both
    )

    two = send(after(pair, mine), along(2))
    from_one = send(after(to_one, mine), along(1))
    theirs = send(mine, chip_swap)
    x_first, y_first = call(
        first_kernel, (coded_two, coded_two), [SM] + [VM] * 3, panel, flops, moved, "first"
    )(table, ancestor_inverse, mine, theirs)
    x_first = send(x_first, across(1))
    y_first = send(y_first, across(2))
    mine = small(pack_kernel, line, "pack_second", pair, after(two, x_first, y_first, from_one))

    theirs = send(mine, chip_swap)
    from_two = send(after(to_two, mine), along(2))
    from_three = send(after(to_three, mine), along(3))
    x_second, y_second, own = call(
        second_kernel,
        (coded, coded, shape((rows, B), f32)),
        [SM] + [VM] * 5,
        panel,
        flops,
        moved,
        "second",
    )(table, ancestor_inverse, mine, theirs, x_first, y_first)
    x_second = send(x_second, across(1))
    y_second = send(y_second, across(2))
    off_inverse, rest = call(
        sum_kernel,
        (shape((rows, B), bf16),) * 2,
        [SM] + [VM] * 5,
        [],
        8 * rows * B,
        12 * rows * B,
        "sum",
    )(table, own, x_first, y_first, x_second, y_second)
    half_rows = shape((2 * shard, B), bf16)
    keep, give = small(
        share_kernel, (half_rows, half_rows), "share", stay, from_one, from_two, from_three
    )
    came = send(give, chip_swap)
    diag = call(
        diag_kernel,
        shape((B, B), f32),
        [VM] * 4,
        [pltpu.VMEM((rows, B), bf16)],
        4 * rows * B * B,
        moved,
        "diag",
    )(off_inverse, rest, keep, came)

    half, part = B // 2, B // 8
    total = diag[:half] + send(diag[half:], chip_swap)
    total = total[: 2 * part] + send(total[2 * part :], along(2))
    total = total[:part] + send(total[part:], along(1))
    return off_inverse, pivot_inverse - total


def body(ancestor_inverse, lower_panel, pivot_inverse, struct_list):
    rows, depth = ancestor_inverse.shape
    shard = lower_panel.shape[0]
    line = (
        lax.axis_size("prow") == 4
        and lax.axis_size("pcol") == 8
        and depth == 8 * shard
        and depth == 2 * rows
        and shard % 64 == 0
        and shard <= B
    )
    plan = line_body if line else general_body
    return plan(ancestor_inverse, lower_panel, pivot_inverse, struct_list)


def solution(mesh):
    placed = (P("pcol", "prow"), P(("prow", "pcol"), None), P("pcol", "prow"), P())
    return jax.shard_map(
        body,
        mesh=mesh,
        in_specs=placed,
        out_specs=(P("pcol", "prow"), P("pcol", "prow")),
        check_vma=False,
    )
```

```python
import functools

import jax
import jax.numpy as jnp
from jax import lax
from jax.experimental import pallas as pl
from jax.experimental.pallas import tpu as pltpu
from jax.sharding import PartitionSpec as P

B = 256
NK = 4
AXES = ("prow", "pcol")
TAIL = 16


def from_root(value, axis, root):
    mine = lax.axis_index(axis) == root
    return lax.psum(jnp.where(mine, value, jnp.zeros_like(value)), axis)


def membership(struct_list, ancestor_ids):
    listed = struct_list[:, :, None] == ancestor_ids[None, None, :]
    return jnp.transpose(jnp.any(listed, axis=1))


def general_body(ancestor_inverse, lower_panel, pivot_inverse, struct_list):
    row_count = ancestor_inverse.shape[0] // B
    col_count = ancestor_inverse.shape[1] // B
    grid_rows = lax.axis_size("prow")
    prow_index = lax.axis_index("prow")
    pcol_index = lax.axis_index("pcol")
    col_share = NK * B // grid_rows
    gathered = lax.all_gather(lower_panel, "pcol", axis=0, tiled=True)
    col_ids = prow_index * col_count + jnp.arange(col_count, dtype=jnp.int32)
    row_ids = pcol_index * row_count + jnp.arange(row_count, dtype=jnp.int32)
    member_cols = membership(struct_list, col_ids)
    member_rows = membership(struct_list, row_ids)
    scaled = gathered.reshape(col_count, B, NK, B) * member_cols[:, None, :, None].astype(
        jnp.bfloat16
    )
    masked = scaled.reshape(col_count * B, NK * B)
    partial_value = -jnp.dot(ancestor_inverse, masked, preferred_element_type=jnp.float32)
    share_sum = lax.psum_scatter(partial_value, "prow", scatter_dimension=1, tiled=True)
    columns = prow_index * col_share + jnp.arange(col_share, dtype=jnp.int32)
    block_of = columns // B
    one_hot = block_of[:, None] == jnp.arange(NK, dtype=jnp.int32)[None, :]
    row_mask = jnp.any(member_rows[:, None, :] & one_hot[None, :, :], axis=2).astype(jnp.float32)
    off_share = (share_sum.reshape(row_count, B, col_share) * row_mask[:, None, :]).reshape(
        row_count * B, col_share
    )
    off_inverse = off_share.astype(jnp.bfloat16)
    block_count = max(col_share // B, 1)
    column_width = col_share // block_count
    offset_blocks = pcol_index * row_count % col_count
    root_row = pcol_index * row_count // col_count
    piece = lax.dynamic_slice_in_dim(masked, offset_blocks * B, row_count * B, 0)
    lower_rows = from_root(piece, "prow", root_row)
    first_block = prow_index * col_share // B
    lower_slice = lax.dynamic_slice_in_dim(lower_rows, first_block * B, block_count * B, 1)
    lower_blocks = lower_slice.astype(jnp.float32).reshape(row_count * B, block_count, B)
    off_blocks = off_share.reshape(row_count * B, block_count, column_width)
    diag_term = jnp.einsum(
        "ikr,ikc->rkc", lower_blocks, off_blocks, precision=lax.Precision.HIGHEST
    ).reshape(B, col_share)
    diag_share = lax.psum_scatter(diag_term, "pcol", scatter_dimension=0, tiled=True)
    diag_inverse = pivot_inverse - diag_share
    return (off_inverse, diag_inverse)


VM = pl.BlockSpec(memory_space=pltpu.VMEM)
SM = pl.BlockSpec(memory_space=pltpu.SMEM)
FINE = 64
FILL = 0.9999


def place():
    p = lax.axis_index("prow")
    q = lax.axis_index("pcol")
    return p, q // 2, q % 2


def call(kernel, outs, specs, scratch, flops, moved, name, room=2**23):
    return pl.pallas_call(
        kernel,
        out_shape=outs,
        in_specs=specs,
        out_specs=jax.tree.map(lambda _: VM, outs),
        scratch_shapes=scratch,
        compiler_params=pltpu.CompilerParams(vmem_limit_bytes=room),
        cost_estimate=pl.CostEstimate(flops=flops, bytes_accessed=moved, transcendentals=0),
        name=name,
    )


def is_member(struct_ref, level, ancestor):
    found = struct_ref[level, 0] == ancestor
    for slot in range(1, struct_ref.shape[1]):
        found = found | (struct_ref[level, slot] == ancestor)
    return found


def column_power(value):
    top = jnp.maximum(jnp.max(jnp.abs(value), axis=0, keepdims=True), 2e-34)
    power = jnp.floor(jnp.log2(top)) + 1.0
    return jnp.where(top >= jnp.exp2(power), power + 1.0, power)


def put_tail(ref, powers, rows):
    row = lax.broadcasted_iota(jnp.int32, (TAIL, ref.shape[1]), 0)
    tail = jnp.zeros((TAIL, ref.shape[1]), jnp.float32)
    for block, power in enumerate(powers):
        tail = jnp.where(row == block, power, tail)
    ref[rows : rows + TAIL] = tail.astype(jnp.int32).astype(jnp.int16)


def to_code(value):
    return jnp.round(value).astype(jnp.int32).astype(jnp.int16)


def from_code(code):
    return code.astype(jnp.int32).astype(jnp.float32)


def code_kernel(lower_ref, code_ref, own, to_x, to_y, to_both):
    p, _, _ = place()
    shard = lower_ref.shape[0]

    def level(k):
        return lower_ref[:, pl.ds(pl.multiple_of(k * B, B), B)]

    for flip, out in enumerate((own, to_x, to_y, to_both)):
        out[...] = level(p ^ flip)
    powers = [[] for _ in range(shard // FINE)]
    for slot, flip in enumerate((3, 1, 2, 0)):
        value = level(p ^ flip).astype(jnp.float32)
        for i in range(shard // FINE):
            rows = slice(i * FINE, (i + 1) * FINE)
            power = column_power(value[rows])
            code_ref[rows, slot * B : (slot + 1) * B] = to_code(
                value[rows] * jnp.exp2(15.0 - power)
            )
            powers[i].append(power)
    put_tail(code_ref, [jnp.concatenate(power, axis=1) for power in powers], shard)


def load_panel(code_ref, panel, struct_ref, slots):
    p, _, _ = place()
    span = code_ref.shape[0] // 8
    shard = span - TAIL
    blocks = panel.shape[0] // B
    for at, (slot, flip) in enumerate(slots):
        lanes = slice(slot * B, (slot + 1) * B)
        for s in range(8):
            last = s * span + shard
            step = jnp.exp2(from_code(code_ref[last : last + TAIL, lanes]) - 15.0)
            for i in range(shard // FINE):
                first = s * span + i * FINE
                value = from_code(code_ref[first : first + FINE, lanes]) * step[i : i + 1]
                row = s * shard + i * FINE
                panel[row : row + FINE, at * B : (at + 1) * B] = value.astype(jnp.bfloat16)
        for block in range(blocks):

            @pl.when(jnp.logical_not(is_member(struct_ref, p ^ flip, p * blocks + block)))
            def _(block=block, at=at):
                panel[block * B : (block + 1) * B, at * B : (at + 1) * B] = jnp.zeros(
                    (B, B), jnp.bfloat16
                )


def sums_kernel(slots, struct_ref, a_ref, code_ref, *refs):
    outs, panel = refs[:-1], refs[-1]
    load_panel(code_ref, panel, struct_ref, slots)
    blocks = a_ref.shape[0] // B
    powers = [[] for _ in outs]
    for b in range(blocks):
        rows = slice(b * B, (b + 1) * B)
        total = -jnp.dot(a_ref[rows], panel[...], preferred_element_type=jnp.float32)
        for i, ref in enumerate(outs):
            part = total[:, i * B : (i + 1) * B]
            power = column_power(part)
            ref[rows] = to_code(part * (jnp.exp2(15.0 - power) * FILL))
            powers[i].append(power)
    for ref, power in zip(outs, powers):
        put_tail(ref, power, blocks * B)


def own_kernel(struct_ref, a_ref, code_ref, own_ref, panel):
    load_panel(code_ref, panel, struct_ref, ((3, 0),))
    own_ref[...] = -jnp.dot(a_ref[...], panel[...], preferred_element_type=jnp.float32)


def route_kernel(own, x, y, both, *outs):
    p, z, _ = place()
    for flip, out in enumerate(outs):
        for turn, ref in enumerate((own, x, y, both)):

            @pl.when((p ^ z) == (turn ^ flip))
            def _(ref=ref, out=out):
                out[...] = ref[...]


def share_kernel(own, one, two, three, keep_ref, give_ref):
    _, z, c = place()
    shard = own.shape[0]
    for flip, ref in enumerate((own, one, two, three)):
        chip = z ^ flip
        at = pl.multiple_of((chip % 2) * shard, 64)

        @pl.when(chip // 2 == c)
        def _(ref=ref, at=at):
            keep_ref[pl.ds(at, shard)] = ref[...]

        @pl.when(chip // 2 != c)
        def _(ref=ref, at=at):
            give_ref[pl.ds(at, shard)] = ref[...]


def turn_kernel(keep, came, out_ref, lower):
    _, _, c = place()
    shard = keep.shape[0] // 2
    for half in range(2):
        for ref, core in ((keep, c), (came, 1 - c)):
            at = pl.multiple_of((2 * half + core) * shard, FINE)
            lower[pl.ds(at, shard)] = ref[half * shard : (half + 1) * shard]
    out_ref[...] = jnp.transpose(lower[...])


def last_kernel(
    struct_ref, own_ref, came_d, came_x, came_y, lower, off_ref, diag_ref, both
):
    p, z, c = place()
    blocks = off_ref.shape[0] // B
    first = (2 * z + c) * blocks
    steps = [
        jnp.exp2(from_code(ref[blocks * B : blocks * B + TAIL]) - 15.0) * (1.0 / FILL)
        for ref in (came_d, came_x, came_y)
    ]
    for b in range(blocks):
        rows = slice(b * B, (b + 1) * B)
        total = own_ref[rows]
        for ref, step in zip((came_d, came_x, came_y), steps):
            total = total + from_code(ref[rows]) * step[b : b + 1]
        total = jnp.where(is_member(struct_ref, p, first + b), total, 0.0)
        high = total.astype(jnp.bfloat16)
        off_ref[rows] = high
        both[rows, :B] = high
        both[rows, B:] = (total - high.astype(jnp.float32)).astype(jnp.bfloat16)
    diag = jnp.dot(lower[...], both[...], preferred_element_type=jnp.float32)
    diag = diag[:, :B] + diag[:, B:]
    piece = B // 8
    for zz in range(4):
        for cc in range(2):
            slot = (cc ^ c) * 4 + (zz ^ z)
            at = (2 * zz + cc) * piece
            diag_ref[pl.ds(pl.multiple_of(slot * piece, piece), piece)] = diag[at : at + piece]


def send(value, move):
    found = []
    for p in range(4):
        for z in range(4):
            for c in range(2):
                to = move(p, z, c)
                found.append((p * 8 + 2 * z + c, to[0] * 8 + 2 * to[1] + to[2]))
    return lax.ppermute(value, AXES, found)


def chip_swap(p, z, c):
    return (p, z, 1 - c)


def along(flip):
    return lambda p, z, c: (p, z ^ flip, c)


def across(flip):
    return lambda p, z, c: (p ^ flip, z, c)


def after(value, *earlier):
    return lax.optimization_barrier((value, *earlier))[0]


def line_body(ancestor_inverse, lower_panel, pivot_inverse, struct_list):
    rows, depth = ancestor_inverse.shape
    shard = lower_panel.shape[0]
    bf16, f32, i16 = jnp.bfloat16, jnp.float32, jnp.int16
    shape = jax.ShapeDtypeStruct
    piece = shape((shard, B), bf16)
    code, keep, to_x, to_y, to_both = call(
        code_kernel,
        (shape((shard + TAIL, NK * B), i16),) + (piece,) * 4,
        [VM],
        [],
        8 * shard * NK * B,
        4 * shard * NK * B,
        "code",
    )(lower_panel)
    rows_x = send(to_x, across(1))
    rows_y = send(to_y, across(2))
    rows_both = send(to_both, across(3))
    gathered = lax.all_gather(code, "pcol", axis=0, tiled=True)

    coded = shape((rows + TAIL, B), i16)

    def sums(slots, outs, name, *args):
        return call(
            functools.partial(sums_kernel, slots),
            (coded,) * outs,
            [SM, VM, VM],
            [pltpu.VMEM((depth, outs * B), bf16)],
            1,
            1,
            name,
        )(*args)

    (part_d,) = sums(((0, 3),), 1, "sums_d", struct_list, ancestor_inverse, gathered)
    came_d = send(part_d, across(3))
    part_x, part_y = sums(
        ((1, 1), (2, 2)), 2, "sums_xy", after(struct_list, part_d), ancestor_inverse, gathered
    )
    came_x = send(part_x, across(1))
    came_y = send(part_y, across(2))
    def small(kernel, outs, name, *args):
        return call(kernel, outs, [VM] * len(args), [], 1, 1, name, room=2**21)(*args)

    stay, to_one, to_two, to_three = small(
        route_kernel, (piece,) * 4, "route", keep, rows_x, rows_y, rows_both
    )
    from_one = send(to_one, along(1))
    from_two = send(to_two, along(2))
    from_three = send(to_three, along(3))
    half_rows = shape((2 * shard, B), bf16)
    keep, give = small(
        share_kernel, (half_rows, half_rows), "share", stay, from_one, from_two, from_three
    )
    lower = call(
        turn_kernel,
        shape((B, rows), bf16),
        [VM, VM],
        [pltpu.VMEM((rows, B), bf16)],
        1,
        1,
        "turn",
    )(keep, send(give, chip_swap))
    own = call(
        own_kernel,
        shape((rows, B), f32),
        [SM, VM, VM],
        [pltpu.VMEM((depth, B), bf16)],
        1,
        1,
        "own",
    )(after(struct_list, part_x), ancestor_inverse, gathered)
    off_inverse, diag = call(
        last_kernel,
        (shape((rows, B), bf16), shape((B, B), f32)),
        [SM] + [VM] * 5,
        [pltpu.VMEM((rows, 2 * B), bf16)],
        4 * rows * B * B,
        8 * rows * B,
        "last",
    )(struct_list, own, came_d, came_x, came_y, lower)

    half, part = B // 2, B // 8
    total = diag[:half] + send(diag[half:], chip_swap)
    near = [send(total[i * part : (i + 1) * part], along(i)) for i in (1, 2, 3)]
    return off_inverse, pivot_inverse - (total[:part] + near[0] + near[1] + near[2])


def body(ancestor_inverse, lower_panel, pivot_inverse, struct_list):
    rows, depth = ancestor_inverse.shape
    shard = lower_panel.shape[0]
    line = (
        lax.axis_size("prow") == 4
        and lax.axis_size("pcol") == 8
        and depth == 8 * shard
        and depth == 2 * rows
        and shard % 64 == 0
        and shard <= B
    )
    plan = line_body if line else general_body
    return plan(ancestor_inverse, lower_panel, pivot_inverse, struct_list)


def solution(mesh):
    placed = (P("pcol", "prow"), P(("prow", "pcol"), None), P("pcol", "prow"), P())
    return jax.shard_map(
        body,
        mesh=mesh,
        in_specs=placed,
        out_specs=(P("pcol", "prow"), P("pcol", "prow")),
        check_vma=False,
    )
```

```python
import functools

import jax
import jax.numpy as jnp
from jax import lax
from jax.experimental import pallas as pl
from jax.experimental.pallas import tpu as pltpu
from jax.sharding import PartitionSpec as P

B = 256
NK = 4
AXES = ("prow", "pcol")
TAIL = 16


def from_root(value, axis, root):
    mine = lax.axis_index(axis) == root
    return lax.psum(jnp.where(mine, value, jnp.zeros_like(value)), axis)


def membership(struct_list, ancestor_ids):
    listed = struct_list[:, :, None] == ancestor_ids[None, None, :]
    return jnp.transpose(jnp.any(listed, axis=1))


def general_body(ancestor_inverse, lower_panel, pivot_inverse, struct_list):
    row_count = ancestor_inverse.shape[0] // B
    col_count = ancestor_inverse.shape[1] // B
    grid_rows = lax.axis_size("prow")
    prow_index = lax.axis_index("prow")
    pcol_index = lax.axis_index("pcol")
    col_share = NK * B // grid_rows
    gathered = lax.all_gather(lower_panel, "pcol", axis=0, tiled=True)
    col_ids = prow_index * col_count + jnp.arange(col_count, dtype=jnp.int32)
    row_ids = pcol_index * row_count + jnp.arange(row_count, dtype=jnp.int32)
    member_cols = membership(struct_list, col_ids)
    member_rows = membership(struct_list, row_ids)
    scaled = gathered.reshape(col_count, B, NK, B) * member_cols[:, None, :, None].astype(
        jnp.bfloat16
    )
    masked = scaled.reshape(col_count * B, NK * B)
    partial_value = -jnp.dot(ancestor_inverse, masked, preferred_element_type=jnp.float32)
    share_sum = lax.psum_scatter(partial_value, "prow", scatter_dimension=1, tiled=True)
    columns = prow_index * col_share + jnp.arange(col_share, dtype=jnp.int32)
    block_of = columns // B
    one_hot = block_of[:, None] == jnp.arange(NK, dtype=jnp.int32)[None, :]
    row_mask = jnp.any(member_rows[:, None, :] & one_hot[None, :, :], axis=2).astype(jnp.float32)
    off_share = (share_sum.reshape(row_count, B, col_share) * row_mask[:, None, :]).reshape(
        row_count * B, col_share
    )
    off_inverse = off_share.astype(jnp.bfloat16)
    block_count = max(col_share // B, 1)
    column_width = col_share // block_count
    offset_blocks = pcol_index * row_count % col_count
    root_row = pcol_index * row_count // col_count
    piece = lax.dynamic_slice_in_dim(masked, offset_blocks * B, row_count * B, 0)
    lower_rows = from_root(piece, "prow", root_row)
    first_block = prow_index * col_share // B
    lower_slice = lax.dynamic_slice_in_dim(lower_rows, first_block * B, block_count * B, 1)
    lower_blocks = lower_slice.astype(jnp.float32).reshape(row_count * B, block_count, B)
    off_blocks = off_share.reshape(row_count * B, block_count, column_width)
    diag_term = jnp.einsum(
        "ikr,ikc->rkc", lower_blocks, off_blocks, precision=lax.Precision.HIGHEST
    ).reshape(B, col_share)
    diag_share = lax.psum_scatter(diag_term, "pcol", scatter_dimension=0, tiled=True)
    diag_inverse = pivot_inverse - diag_share
    return (off_inverse, diag_inverse)


VM = pl.BlockSpec(memory_space=pltpu.VMEM)
SM = pl.BlockSpec(memory_space=pltpu.SMEM)
FINE = 64
TINY = 2.0**-100
FILL = 0.9999


def place():
    p = lax.axis_index("prow")
    q = lax.axis_index("pcol")
    return p, q // 2, q % 2


def call(kernel, outs, specs, scratch, flops, moved, name, room=2**23):
    return pl.pallas_call(
        kernel,
        out_shape=outs,
        in_specs=specs,
        out_specs=jax.tree.map(lambda _: VM, outs),
        scratch_shapes=scratch,
        compiler_params=pltpu.CompilerParams(vmem_limit_bytes=room),
        cost_estimate=pl.CostEstimate(flops=flops, bytes_accessed=moved, transcendentals=0),
        name=name,
    )


def is_member(struct_ref, level, ancestor):
    found = struct_ref[level, 0] == ancestor
    for slot in range(1, struct_ref.shape[1]):
        found = found | (struct_ref[level, slot] == ancestor)
    return found


def column_power(value):
    top = jnp.maximum(jnp.max(jnp.abs(value), axis=0, keepdims=True), 2e-34)
    power = jnp.floor(jnp.log2(top)) + 1.0
    return jnp.where(top >= jnp.exp2(power), power + 1.0, power)


def put_tail(ref, powers, rows):
    row = lax.broadcasted_iota(jnp.int32, (TAIL, ref.shape[1]), 0)
    tail = jnp.zeros((TAIL, ref.shape[1]), jnp.float32)
    for block, power in enumerate(powers):
        tail = jnp.where(row == block, power, tail)
    ref[rows : rows + TAIL] = tail.astype(jnp.int32).astype(jnp.int16)


def to_code(value):
    return jnp.round(value).astype(jnp.int32).astype(jnp.int16)


def from_code(code):
    return code.astype(jnp.int32).astype(jnp.float32)


def code_kernel(lower_ref, code_ref, own, to_x, to_y, to_both):
    p, _, _ = place()

    def level(k):
        return lower_ref[:, pl.ds(pl.multiple_of(k * B, B), B)]

    for flip, out in enumerate((own, to_x, to_y, to_both)):
        out[...] = level(p ^ flip)
    for slot, flip in enumerate((3, 1, 2, 0)):
        value = level(p ^ flip).astype(jnp.float32)
        size = jnp.abs(value)
        power = jnp.floor(jnp.log2(jnp.maximum(size, TINY)))
        code = jnp.round(size * jnp.exp2(7.0 - power)) + (power + 126.0) * 128.0
        code = jnp.where(size < TINY, 0.0, jnp.where(value < 0.0, -code, code))
        code_ref[:, slot * B : (slot + 1) * B] = code.astype(jnp.int32).astype(jnp.int16)


def load_panel(code_ref, panel, struct_ref, slots):
    p, _, _ = place()
    blocks = panel.shape[0] // B
    for at, (slot, flip) in enumerate(slots):
        for block in range(blocks):
            rows = slice(block * B, (block + 1) * B)
            listed = is_member(struct_ref, p ^ flip, p * blocks + block)

            @pl.when(listed)
            def _(rows=rows, at=at, slot=slot):
                code = code_ref[rows, slot * B : (slot + 1) * B].astype(jnp.int32)
                size = jnp.abs(code)
                power = jnp.exp2(((size >> 7) - 134).astype(jnp.float32))
                value = ((size & 127) + 128).astype(jnp.float32) * power
                panel[rows, at * B : (at + 1) * B] = jnp.where(code < 0, -value, value).astype(
                    jnp.bfloat16
                )

            @pl.when(jnp.logical_not(listed))
            def _(rows=rows, at=at):
                panel[rows, at * B : (at + 1) * B] = jnp.zeros((B, B), jnp.bfloat16)


def sums_kernel(slots, struct_ref, a_ref, code_ref, *refs):
    outs, panel = refs[:-1], refs[-1]
    load_panel(code_ref, panel, struct_ref, slots)
    blocks = a_ref.shape[0] // B
    powers = [[] for _ in outs]
    for b in range(blocks):
        rows = slice(b * B, (b + 1) * B)
        total = -jnp.dot(a_ref[rows], panel[...], preferred_element_type=jnp.float32)
        for i, ref in enumerate(outs):
            part = total[:, i * B : (i + 1) * B]
            power = column_power(part)
            ref[rows] = to_code(part * (jnp.exp2(15.0 - power) * FILL))
            powers[i].append(power)
    for ref, power in zip(outs, powers):
        put_tail(ref, power, blocks * B)


def came_step(ref, blocks):
    return jnp.exp2(from_code(ref[blocks * B : blocks * B + TAIL]) - 15.0) * (1.0 / FILL)


def own_kernel(struct_ref, a_ref, code_ref, came_d, own_ref, panel):
    load_panel(code_ref, panel, struct_ref, ((3, 0),))
    blocks = own_ref.shape[0] // B
    step = came_step(came_d, blocks)
    for b in range(blocks):
        rows = slice(b * B, (b + 1) * B)
        own_ref[rows] = from_code(came_d[rows]) * step[b : b + 1] - jnp.dot(
            a_ref[rows], panel[...], preferred_element_type=jnp.float32
        )


def route_kernel(own, x, y, both, *outs):
    p, z, _ = place()
    for flip, out in enumerate(outs):
        for turn, ref in enumerate((own, x, y, both)):

            @pl.when((p ^ z) == (turn ^ flip))
            def _(ref=ref, out=out):
                out[...] = ref[...]


def share_kernel(own, one, two, three, keep_ref, give_ref):
    _, z, c = place()
    shard = own.shape[0]
    for flip, ref in enumerate((own, one, two, three)):
        chip = z ^ flip
        at = pl.multiple_of((chip % 2) * shard, 64)

        @pl.when(chip // 2 == c)
        def _(ref=ref, at=at):
            keep_ref[pl.ds(at, shard)] = ref[...]

        @pl.when(chip // 2 != c)
        def _(ref=ref, at=at):
            give_ref[pl.ds(at, shard)] = ref[...]


def turn_kernel(keep, came, out_ref, lower):
    _, _, c = place()
    shard = keep.shape[0] // 2
    for half in range(2):
        for ref, core in ((keep, c), (came, 1 - c)):
            at = pl.multiple_of((2 * half + core) * shard, FINE)
            lower[pl.ds(at, shard)] = ref[half * shard : (half + 1) * shard]
    out_ref[...] = jnp.transpose(lower[...])


def last_kernel(
    struct_ref, own_ref, came_x, came_y, lower, off_ref, diag_ref, both
):
    p, z, c = place()
    blocks = off_ref.shape[0] // B
    first = (2 * z + c) * blocks
    steps = [came_step(ref, blocks) for ref in (came_x, came_y)]
    for b in range(blocks):
        rows = slice(b * B, (b + 1) * B)
        total = own_ref[rows]
        for ref, step in zip((came_x, came_y), steps):
            total = total + from_code(ref[rows]) * step[b : b + 1]
        total = jnp.where(is_member(struct_ref, p, first + b), total, 0.0)
        high = total.astype(jnp.bfloat16)
        off_ref[rows] = high
        both[rows, :B] = high
        both[rows, B:] = (total - high.astype(jnp.float32)).astype(jnp.bfloat16)
    diag = jnp.dot(lower[...], both[...], preferred_element_type=jnp.float32)
    diag = diag[:, :B] + diag[:, B:]
    piece = B // 8
    for zz in range(4):
        for cc in range(2):
            slot = (cc ^ c) * 4 + (zz ^ z)
            at = (2 * zz + cc) * piece
            diag_ref[pl.ds(pl.multiple_of(slot * piece, piece), piece)] = diag[at : at + piece]


def send(value, move):
    found = []
    for p in range(4):
        for z in range(4):
            for c in range(2):
                to = move(p, z, c)
                found.append((p * 8 + 2 * z + c, to[0] * 8 + 2 * to[1] + to[2]))
    return lax.ppermute(value, AXES, found)


def chip_swap(p, z, c):
    return (p, z, 1 - c)


def along(flip):
    return lambda p, z, c: (p, z ^ flip, c)


def across(flip):
    return lambda p, z, c: (p ^ flip, z, c)


def after(value, *earlier):
    return lax.optimization_barrier((value, *earlier))[0]


def line_body(ancestor_inverse, lower_panel, pivot_inverse, struct_list):
    rows, depth = ancestor_inverse.shape
    shard = lower_panel.shape[0]
    bf16, f32, i16 = jnp.bfloat16, jnp.float32, jnp.int16
    shape = jax.ShapeDtypeStruct
    piece = shape((shard, B), bf16)
    code, keep, to_x, to_y, to_both = call(
        code_kernel,
        (shape((shard, NK * B), i16),) + (piece,) * 4,
        [VM],
        [],
        8 * shard * NK * B,
        4 * shard * NK * B,
        "code",
    )(lower_panel)
    rows_x = send(to_x, across(1))
    rows_y = send(to_y, across(2))
    rows_both = send(to_both, across(3))
    gathered = lax.all_gather(code, "pcol", axis=0, tiled=True)

    coded = shape((rows + TAIL, B), i16)

    def sums(slots, outs, name, *args):
        return call(
            functools.partial(sums_kernel, slots),
            (coded,) * outs,
            [SM, VM, VM],
            [pltpu.VMEM((depth, outs * B), bf16)],
            1,
            1,
            name,
        )(*args)

    (part_d,) = sums(((0, 3),), 1, "sums_d", struct_list, ancestor_inverse, gathered)
    came_d = send(part_d, across(3))
    part_x, part_y = sums(
        ((1, 1), (2, 2)), 2, "sums_xy", after(struct_list, part_d), ancestor_inverse, gathered
    )
    came_x = send(part_x, across(1))
    came_y = send(part_y, across(2))
    def small(kernel, outs, name, *args, flops=1):
        return call(kernel, outs, [VM] * len(args), [], flops, 1, name, room=2**21)(*args)

    stay, to_one, to_two, to_three = small(
        route_kernel, (piece,) * 4, "route", keep, rows_x, rows_y, rows_both, flops=1
    )
    from_one = send(to_one, along(1))
    from_two = send(to_two, along(2))
    from_three = send(after(to_three, from_one), along(3))
    own = call(
        own_kernel,
        shape((rows, B), f32),
        [SM, VM, VM, VM],
        [pltpu.VMEM((depth, B), bf16)],
        1,
        1,
        "own",
    )(struct_list, ancestor_inverse, gathered, came_d)
    half_rows = shape((2 * shard, B), bf16)
    keep, give = small(
        share_kernel, (half_rows, half_rows), "share", stay, from_one, from_two, from_three
    )
    lower = call(
        turn_kernel,
        shape((B, rows), bf16),
        [VM, VM],
        [pltpu.VMEM((rows, B), bf16)],
        1,
        1,
        "turn",
    )(keep, send(give, chip_swap))
    off_inverse, diag = call(
        last_kernel,
        (shape((rows, B), bf16), shape((B, B), f32)),
        [SM] + [VM] * 4,
        [pltpu.VMEM((rows, 2 * B), bf16)],
        4 * rows * B * B,
        8 * rows * B,
        "last",
    )(struct_list, own, came_x, came_y, lower)

    half, part = B // 2, B // 8
    total = diag[:half] + send(diag[half:], chip_swap)
    near = [send(total[i * part : (i + 1) * part], along(i)) for i in (1, 2, 3)]
    return off_inverse, pivot_inverse - (total[:part] + near[0] + near[1] + near[2])


def body(ancestor_inverse, lower_panel, pivot_inverse, struct_list):
    rows, depth = ancestor_inverse.shape
    shard = lower_panel.shape[0]
    line = (
        lax.axis_size("prow") == 4
        and lax.axis_size("pcol") == 8
        and depth == 8 * shard
        and depth == 2 * rows
        and shard % 64 == 0
        and shard <= B
    )
    plan = line_body if line else general_body
    return plan(ancestor_inverse, lower_panel, pivot_inverse, struct_list)


def solution(mesh):
    placed = (P("pcol", "prow"), P(("prow", "pcol"), None), P("pcol", "prow"), P())
    return jax.shard_map(
        body,
        mesh=mesh,
        in_specs=placed,
        out_specs=(P("pcol", "prow"), P("pcol", "prow")),
        check_vma=False,
    )
```

```python
import functools

import jax
import jax.numpy as jnp
from jax import lax
from jax.experimental import pallas as pl
from jax.experimental.pallas import tpu as pltpu
from jax.sharding import PartitionSpec as P

B = 256
NK = 4
AXES = ("prow", "pcol")
TAIL = 16


def from_root(value, axis, root):
    mine = lax.axis_index(axis) == root
    return lax.psum(jnp.where(mine, value, jnp.zeros_like(value)), axis)


def membership(struct_list, ancestor_ids):
    listed = struct_list[:, :, None] == ancestor_ids[None, None, :]
    return jnp.transpose(jnp.any(listed, axis=1))


def general_body(ancestor_inverse, lower_panel, pivot_inverse, struct_list):
    row_count = ancestor_inverse.shape[0] // B
    col_count = ancestor_inverse.shape[1] // B
    grid_rows = lax.axis_size("prow")
    prow_index = lax.axis_index("prow")
    pcol_index = lax.axis_index("pcol")
    col_share = NK * B // grid_rows
    gathered = lax.all_gather(lower_panel, "pcol", axis=0, tiled=True)
    col_ids = prow_index * col_count + jnp.arange(col_count, dtype=jnp.int32)
    row_ids = pcol_index * row_count + jnp.arange(row_count, dtype=jnp.int32)
    member_cols = membership(struct_list, col_ids)
    member_rows = membership(struct_list, row_ids)
    scaled = gathered.reshape(col_count, B, NK, B) * member_cols[:, None, :, None].astype(
        jnp.bfloat16
    )
    masked = scaled.reshape(col_count * B, NK * B)
    partial_value = -jnp.dot(ancestor_inverse, masked, preferred_element_type=jnp.float32)
    share_sum = lax.psum_scatter(partial_value, "prow", scatter_dimension=1, tiled=True)
    columns = prow_index * col_share + jnp.arange(col_share, dtype=jnp.int32)
    block_of = columns // B
    one_hot = block_of[:, None] == jnp.arange(NK, dtype=jnp.int32)[None, :]
    row_mask = jnp.any(member_rows[:, None, :] & one_hot[None, :, :], axis=2).astype(jnp.float32)
    off_share = (share_sum.reshape(row_count, B, col_share) * row_mask[:, None, :]).reshape(
        row_count * B, col_share
    )
    off_inverse = off_share.astype(jnp.bfloat16)
    block_count = max(col_share // B, 1)
    column_width = col_share // block_count
    offset_blocks = pcol_index * row_count % col_count
    root_row = pcol_index * row_count // col_count
    piece = lax.dynamic_slice_in_dim(masked, offset_blocks * B, row_count * B, 0)
    lower_rows = from_root(piece, "prow", root_row)
    first_block = prow_index * col_share // B
    lower_slice = lax.dynamic_slice_in_dim(lower_rows, first_block * B, block_count * B, 1)
    lower_blocks = lower_slice.astype(jnp.float32).reshape(row_count * B, block_count, B)
    off_blocks = off_share.reshape(row_count * B, block_count, column_width)
    diag_term = jnp.einsum(
        "ikr,ikc->rkc", lower_blocks, off_blocks, precision=lax.Precision.HIGHEST
    ).reshape(B, col_share)
    diag_share = lax.psum_scatter(diag_term, "pcol", scatter_dimension=0, tiled=True)
    diag_inverse = pivot_inverse - diag_share
    return (off_inverse, diag_inverse)


VM = pl.BlockSpec(memory_space=pltpu.VMEM)
SM = pl.BlockSpec(memory_space=pltpu.SMEM)
FINE = 64
TINY = 2.0**-100
FILL = 0.9999


def place():
    p = lax.axis_index("prow")
    q = lax.axis_index("pcol")
    return p, q // 2, q % 2


def call(kernel, outs, specs, scratch, flops, moved, name, room=2**23):
    return pl.pallas_call(
        kernel,
        out_shape=outs,
        in_specs=specs,
        out_specs=jax.tree.map(lambda _: VM, outs),
        scratch_shapes=scratch,
        compiler_params=pltpu.CompilerParams(vmem_limit_bytes=room),
        cost_estimate=pl.CostEstimate(flops=flops, bytes_accessed=moved, transcendentals=0),
        name=name,
    )


def is_member(struct_ref, level, ancestor):
    found = struct_ref[level, 0] == ancestor
    for slot in range(1, struct_ref.shape[1]):
        found = found | (struct_ref[level, slot] == ancestor)
    return found


def column_power(value):
    top = jnp.maximum(jnp.max(jnp.abs(value), axis=0, keepdims=True), 2e-34)
    power = jnp.floor(jnp.log2(top)) + 1.0
    return jnp.where(top >= jnp.exp2(power), power + 1.0, power)


def put_tail(ref, powers, rows):
    row = lax.broadcasted_iota(jnp.int32, (TAIL, ref.shape[1]), 0)
    tail = jnp.zeros((TAIL, ref.shape[1]), jnp.float32)
    for block, power in enumerate(powers):
        tail = jnp.where(row == block, power, tail)
    ref[rows : rows + TAIL] = tail.astype(jnp.int32).astype(jnp.int16)


def to_code(value):
    return jnp.round(value).astype(jnp.int32).astype(jnp.int16)


def from_code(code):
    return code.astype(jnp.int32).astype(jnp.float32)


def code_kernel(lower_ref, code_ref, own, to_x, to_y, to_both):
    p, _, _ = place()

    def level(k):
        return lower_ref[:, pl.ds(pl.multiple_of(k * B, B), B)]

    for flip, out in enumerate((own, to_x, to_y, to_both)):
        out[...] = level(p ^ flip)
    for slot, flip in enumerate((3, 1, 2)):
        value = level(p ^ flip).astype(jnp.float32)
        size = jnp.abs(value)
        power = jnp.floor(jnp.log2(jnp.maximum(size, TINY)))
        code = jnp.round(size * jnp.exp2(7.0 - power)) + (power + 126.0) * 128.0
        code = jnp.where(size < TINY, 0.0, jnp.where(value < 0.0, -code, code))
        code_ref[:, slot * B : (slot + 1) * B] = code.astype(jnp.int32).astype(jnp.int16)


def load_panel(code_ref, panel, struct_ref, slots):
    p, _, _ = place()
    blocks = panel.shape[0] // B
    for at, (slot, flip) in enumerate(slots):
        for block in range(blocks):
            rows = slice(block * B, (block + 1) * B)
            listed = is_member(struct_ref, p ^ flip, p * blocks + block)

            @pl.when(listed)
            def _(rows=rows, at=at, slot=slot):
                code = code_ref[rows, slot * B : (slot + 1) * B].astype(jnp.int32)
                size = jnp.abs(code)
                power = jnp.exp2(((size >> 7) - 134).astype(jnp.float32))
                value = ((size & 127) + 128).astype(jnp.float32) * power
                panel[rows, at * B : (at + 1) * B] = jnp.where(code < 0, -value, value).astype(
                    jnp.bfloat16
                )

            @pl.when(jnp.logical_not(listed))
            def _(rows=rows, at=at):
                panel[rows, at * B : (at + 1) * B] = jnp.zeros((B, B), jnp.bfloat16)


def sums_kernel(slots, struct_ref, a_ref, code_ref, *refs):
    outs, panel = refs[:-1], refs[-1]
    load_panel(code_ref, panel, struct_ref, slots)
    blocks = a_ref.shape[0] // B
    powers = [[] for _ in outs]
    for b in range(blocks):
        rows = slice(b * B, (b + 1) * B)
        total = -jnp.dot(a_ref[rows], panel[...], preferred_element_type=jnp.float32)
        for i, ref in enumerate(outs):
            part = total[:, i * B : (i + 1) * B]
            power = column_power(part)
            ref[rows] = to_code(part * (jnp.exp2(15.0 - power) * FILL))
            powers[i].append(power)
    for ref, power in zip(outs, powers):
        put_tail(ref, power, blocks * B)


def came_step(ref, blocks):
    return jnp.exp2(from_code(ref[blocks * B : blocks * B + TAIL]) - 15.0) * (1.0 / FILL)


def pair_kernel(to_two, own_ref, one_ref, out_ref):
    shard = own_ref.shape[0]
    for at, ref in enumerate((to_two, own_ref, one_ref)):
        out_ref[at * shard : (at + 1) * shard] = ref[...]


def base_kernel(came_ref, base_ref):
    blocks = base_ref.shape[0] // B
    step = came_step(came_ref, blocks)
    for b in range(blocks):
        rows = slice(b * B, (b + 1) * B)
        base_ref[rows] = from_code(came_ref[rows]) * step[b : b + 1]


def own_kernel(
    struct_ref, a_ref, pair, two, their_pair, their_two, base_ref, own_ref, panel
):
    p, z, c = place()
    shard = panel.shape[0] // 8
    for flip in range(4):
        for refs, core in (((pair, two), c), ((their_pair, their_two), 1 - c)):
            at = pl.multiple_of((2 * (z ^ flip) + core) * shard, FINE)
            part = slice((flip % 2) * shard, (flip % 2 + 1) * shard)
            panel[pl.ds(at, shard)] = refs[flip // 2][part]
    blocks = panel.shape[0] // B
    for block in range(blocks):

        @pl.when(jnp.logical_not(is_member(struct_ref, p, p * blocks + block)))
        def _(block=block):
            panel[block * B : (block + 1) * B] = jnp.zeros((B, B), jnp.bfloat16)

    own_ref[...] = base_ref[...] - jnp.dot(
        a_ref[...], panel[...], preferred_element_type=jnp.float32
    )


def route_kernel(own, x, y, both, *outs):
    p, z, _ = place()
    for flip, out in enumerate(outs):
        for turn, ref in enumerate((own, x, y, both)):

            @pl.when((p ^ z) == (turn ^ flip))
            def _(ref=ref, out=out):
                out[...] = ref[...]


def share_kernel(own, one, two, three, keep_ref, give_ref):
    _, z, c = place()
    shard = own.shape[0]
    for flip, ref in enumerate((own, one, two, three)):
        chip = z ^ flip
        at = pl.multiple_of((chip % 2) * shard, 64)

        @pl.when(chip // 2 == c)
        def _(ref=ref, at=at):
            keep_ref[pl.ds(at, shard)] = ref[:shard]

        @pl.when(chip // 2 != c)
        def _(ref=ref, at=at):
            give_ref[pl.ds(at, shard)] = ref[:shard]


def turn_kernel(keep, came, out_ref, lower):
    _, _, c = place()
    shard = keep.shape[0] // 2
    for half in range(2):
        for ref, core in ((keep, c), (came, 1 - c)):
            at = pl.multiple_of((2 * half + core) * shard, FINE)
            lower[pl.ds(at, shard)] = ref[half * shard : (half + 1) * shard]
    out_ref[...] = jnp.transpose(lower[...])


def last_kernel(
    struct_ref, own_ref, came_x, came_y, lower, off_ref, diag_ref, both
):
    p, z, c = place()
    blocks = off_ref.shape[0] // B
    first = (2 * z + c) * blocks
    steps = [came_step(ref, blocks) for ref in (came_x, came_y)]
    for b in range(blocks):
        rows = slice(b * B, (b + 1) * B)
        total = own_ref[rows]
        for ref, step in zip((came_x, came_y), steps):
            total = total + from_code(ref[rows]) * step[b : b + 1]
        total = jnp.where(is_member(struct_ref, p, first + b), total, 0.0)
        high = total.astype(jnp.bfloat16)
        off_ref[rows] = high
        both[rows, :B] = high
        both[rows, B:] = (total - high.astype(jnp.float32)).astype(jnp.bfloat16)
    diag = jnp.dot(lower[...], both[...], preferred_element_type=jnp.float32)
    diag = diag[:, :B] + diag[:, B:]
    piece = B // 8
    for zz in range(4):
        for cc in range(2):
            slot = (cc ^ c) * 4 + (zz ^ z)
            at = (2 * zz + cc) * piece
            diag_ref[pl.ds(pl.multiple_of(slot * piece, piece), piece)] = diag[at : at + piece]


def send(value, move):
    found = []
    for p in range(4):
        for z in range(4):
            for c in range(2):
                to = move(p, z, c)
                found.append((p * 8 + 2 * z + c, to[0] * 8 + 2 * to[1] + to[2]))
    return lax.ppermute(value, AXES, found)


def chip_swap(p, z, c):
    return (p, z, 1 - c)


def along(flip):
    return lambda p, z, c: (p, z ^ flip, c)


def across(flip):
    return lambda p, z, c: (p ^ flip, z, c)


def after(value, *earlier):
    return lax.optimization_barrier((value, *earlier))[0]


def line_body(ancestor_inverse, lower_panel, pivot_inverse, struct_list):
    rows, depth = ancestor_inverse.shape
    shard = lower_panel.shape[0]
    bf16, f32, i16 = jnp.bfloat16, jnp.float32, jnp.int16
    shape = jax.ShapeDtypeStruct
    piece = shape((shard, B), bf16)
    code, keep, to_x, to_y, to_both = call(
        code_kernel,
        (shape((shard, 3 * B), i16),) + (piece,) * 4,
        [VM],
        [],
        8 * shard * NK * B,
        4 * shard * NK * B,
        "code",
    )(lower_panel)
    def small(kernel, outs, name, *args, flops=1):
        return call(kernel, outs, [VM] * len(args), [], flops, 1, name, room=2**21)(*args)

    own_piece = keep
    far_one = send(keep, along(1))
    rows_x = send(to_x, across(1))
    rows_y = send(to_y, across(2))
    rows_both = send(to_both, across(3))
    gathered = lax.all_gather(code, "pcol", axis=0, tiled=True)

    coded = shape((rows + TAIL, B), i16)

    def sums(slots, outs, name, *args):
        return call(
            functools.partial(sums_kernel, slots),
            (coded,) * outs,
            [SM, VM, VM],
            [pltpu.VMEM((depth, outs * B), bf16)],
            1,
            1,
            name,
        )(*args)

    (part_d,) = sums(((0, 3),), 1, "sums_d", struct_list, ancestor_inverse, gathered)
    came_d = send(part_d, across(3))
    part_x, part_y = sums(
        ((1, 1), (2, 2)), 2, "sums_xy", after(struct_list, part_d), ancestor_inverse, gathered
    )
    came_x = send(part_x, across(1))
    came_y = send(part_y, across(2))
    stay, to_one, to_two, to_three = small(
        route_kernel, (piece,) * 4, "route", keep, rows_x, rows_y, rows_both, flops=8 * 10**9
    )
    to_one, to_two, to_three, _ = lax.optimization_barrier((to_one, to_two, to_three, part_d))
    from_one = send(to_one, along(1))
    trio = small(
        pair_kernel, shape((3 * shard, B), bf16), "pair", to_two, own_piece, far_one, flops=3 * 10**9
    )
    from_two = send(trio, along(2))
    pair, two = trio[shard:], from_two[shard:]
    their_pair = send(pair, chip_swap)
    from_three = send(to_three, along(3))
    base = small(base_kernel, shape((rows, B), f32), "base", came_d, flops=4 * 10**9)
    own = call(
        own_kernel,
        shape((rows, B), f32),
        [SM] + [VM] * 6,
        [pltpu.VMEM((depth, B), bf16)],
        1,
        1,
        "own",
    )(struct_list, ancestor_inverse, pair, two, their_pair, send(two, chip_swap), base)
    half_rows = shape((2 * shard, B), bf16)
    keep, give = small(
        share_kernel, (half_rows, half_rows), "share", stay, from_one, from_two, from_three, flops=2 * 10**9
    )
    lower = call(
        turn_kernel,
        shape((B, rows), bf16),
        [VM, VM],
        [pltpu.VMEM((rows, B), bf16)],
        1,
        1,
        "turn",
    )(keep, send(give, chip_swap))
    off_inverse, diag = call(
        last_kernel,
        (shape((rows, B), bf16), shape((B, B), f32)),
        [SM] + [VM] * 4,
        [pltpu.VMEM((rows, 2 * B), bf16)],
        4 * rows * B * B,
        8 * rows * B,
        "last",
    )(struct_list, own, came_x, came_y, lower)

    half, part = B // 2, B // 8
    total = diag[:half] + send(diag[half:], chip_swap)
    near = [send(total[i * part : (i + 1) * part], along(i)) for i in (1, 2, 3)]
    return off_inverse, pivot_inverse - (total[:part] + near[0] + near[1] + near[2])


def body(ancestor_inverse, lower_panel, pivot_inverse, struct_list):
    rows, depth = ancestor_inverse.shape
    shard = lower_panel.shape[0]
    line = (
        lax.axis_size("prow") == 4
        and lax.axis_size("pcol") == 8
        and depth == 8 * shard
        and depth == 2 * rows
        and shard % 64 == 0
        and shard <= B
    )
    plan = line_body if line else general_body
    return plan(ancestor_inverse, lower_panel, pivot_inverse, struct_list)


def solution(mesh):
    placed = (P("pcol", "prow"), P(("prow", "pcol"), None), P("pcol", "prow"), P())
    return jax.shard_map(
        body,
        mesh=mesh,
        in_specs=placed,
        out_specs=(P("pcol", "prow"), P("pcol", "prow")),
        check_vma=False,
    )
```

```python
import functools

import jax
import jax.numpy as jnp
from jax import lax
from jax.experimental import pallas as pl
from jax.experimental.pallas import tpu as pltpu
from jax.sharding import PartitionSpec as P

B = 256
NK = 4
AXES = ("prow", "pcol")
TAIL = 16


def from_root(value, axis, root):
    mine = lax.axis_index(axis) == root
    return lax.psum(jnp.where(mine, value, jnp.zeros_like(value)), axis)


def membership(struct_list, ancestor_ids):
    listed = struct_list[:, :, None] == ancestor_ids[None, None, :]
    return jnp.transpose(jnp.any(listed, axis=1))


def general_body(ancestor_inverse, lower_panel, pivot_inverse, struct_list):
    row_count = ancestor_inverse.shape[0] // B
    col_count = ancestor_inverse.shape[1] // B
    grid_rows = lax.axis_size("prow")
    prow_index = lax.axis_index("prow")
    pcol_index = lax.axis_index("pcol")
    col_share = NK * B // grid_rows
    gathered = lax.all_gather(lower_panel, "pcol", axis=0, tiled=True)
    col_ids = prow_index * col_count + jnp.arange(col_count, dtype=jnp.int32)
    row_ids = pcol_index * row_count + jnp.arange(row_count, dtype=jnp.int32)
    member_cols = membership(struct_list, col_ids)
    member_rows = membership(struct_list, row_ids)
    scaled = gathered.reshape(col_count, B, NK, B) * member_cols[:, None, :, None].astype(
        jnp.bfloat16
    )
    masked = scaled.reshape(col_count * B, NK * B)
    partial_value = -jnp.dot(ancestor_inverse, masked, preferred_element_type=jnp.float32)
    share_sum = lax.psum_scatter(partial_value, "prow", scatter_dimension=1, tiled=True)
    columns = prow_index * col_share + jnp.arange(col_share, dtype=jnp.int32)
    block_of = columns // B
    one_hot = block_of[:, None] == jnp.arange(NK, dtype=jnp.int32)[None, :]
    row_mask = jnp.any(member_rows[:, None, :] & one_hot[None, :, :], axis=2).astype(jnp.float32)
    off_share = (share_sum.reshape(row_count, B, col_share) * row_mask[:, None, :]).reshape(
        row_count * B, col_share
    )
    off_inverse = off_share.astype(jnp.bfloat16)
    block_count = max(col_share // B, 1)
    column_width = col_share // block_count
    offset_blocks = pcol_index * row_count % col_count
    root_row = pcol_index * row_count // col_count
    piece = lax.dynamic_slice_in_dim(masked, offset_blocks * B, row_count * B, 0)
    lower_rows = from_root(piece, "prow", root_row)
    first_block = prow_index * col_share // B
    lower_slice = lax.dynamic_slice_in_dim(lower_rows, first_block * B, block_count * B, 1)
    lower_blocks = lower_slice.astype(jnp.float32).reshape(row_count * B, block_count, B)
    off_blocks = off_share.reshape(row_count * B, block_count, column_width)
    diag_term = jnp.einsum(
        "ikr,ikc->rkc", lower_blocks, off_blocks, precision=lax.Precision.HIGHEST
    ).reshape(B, col_share)
    diag_share = lax.psum_scatter(diag_term, "pcol", scatter_dimension=0, tiled=True)
    diag_inverse = pivot_inverse - diag_share
    return (off_inverse, diag_inverse)


VM = pl.BlockSpec(memory_space=pltpu.VMEM)
SM = pl.BlockSpec(memory_space=pltpu.SMEM)
FINE = 64
TINY = 2.0**-100
FILL = 0.9999


def place():
    p = lax.axis_index("prow")
    q = lax.axis_index("pcol")
    return p, q // 2, q % 2


def call(kernel, outs, specs, scratch, flops, moved, name, room=2**23):
    return pl.pallas_call(
        kernel,
        out_shape=outs,
        in_specs=specs,
        out_specs=jax.tree.map(lambda _: VM, outs),
        scratch_shapes=scratch,
        compiler_params=pltpu.CompilerParams(vmem_limit_bytes=room),
        cost_estimate=pl.CostEstimate(flops=flops, bytes_accessed=moved, transcendentals=0),
        name=name,
    )


def is_member(struct_ref, level, ancestor):
    found = struct_ref[level, 0] == ancestor
    for slot in range(1, struct_ref.shape[1]):
        found = found | (struct_ref[level, slot] == ancestor)
    return found


def column_power(value):
    top = jnp.maximum(jnp.max(jnp.abs(value), axis=0, keepdims=True), 2e-34)
    power = jnp.floor(jnp.log2(top)) + 1.0
    return jnp.where(top >= jnp.exp2(power), power + 1.0, power)


def put_tail(ref, powers, rows):
    row = lax.broadcasted_iota(jnp.int32, (TAIL, ref.shape[1]), 0)
    tail = jnp.zeros((TAIL, ref.shape[1]), jnp.float32)
    for block, power in enumerate(powers):
        tail = jnp.where(row == block, power, tail)
    ref[rows : rows + TAIL] = tail.astype(jnp.int32).astype(jnp.int16)


def to_code(value):
    return jnp.round(value).astype(jnp.int32).astype(jnp.int16)


def from_code(code):
    return code.astype(jnp.int32).astype(jnp.float32)


def code_kernel(lower_ref, code_ref, own, to_x, to_y, to_both):
    p, _, _ = place()

    def level(k):
        return lower_ref[:, pl.ds(pl.multiple_of(k * B, B), B)]

    for flip, out in enumerate((own, to_x, to_y, to_both)):
        out[...] = level(p ^ flip)
    for slot, flip in enumerate((3, 1, 2)):
        value = level(p ^ flip).astype(jnp.float32)
        size = jnp.abs(value)
        power = jnp.floor(jnp.log2(jnp.maximum(size, TINY)))
        code = jnp.round(size * jnp.exp2(7.0 - power)) + (power + 126.0) * 128.0
        code = jnp.where(size < TINY, 0.0, jnp.where(value < 0.0, -code, code))
        code_ref[:, slot * B : (slot + 1) * B] = code.astype(jnp.int32).astype(jnp.int16)


def load_panel(code_ref, panel, struct_ref, slots):
    p, _, _ = place()
    blocks = panel.shape[0] // B
    for at, (slot, flip) in enumerate(slots):
        for block in range(blocks):
            rows = slice(block * B, (block + 1) * B)
            listed = is_member(struct_ref, p ^ flip, p * blocks + block)

            @pl.when(listed)
            def _(rows=rows, at=at, slot=slot):
                code = code_ref[rows, slot * B : (slot + 1) * B].astype(jnp.int32)
                size = jnp.abs(code)
                power = jnp.exp2(((size >> 7) - 134).astype(jnp.float32))
                value = ((size & 127) + 128).astype(jnp.float32) * power
                panel[rows, at * B : (at + 1) * B] = jnp.where(code < 0, -value, value).astype(
                    jnp.bfloat16
                )

            @pl.when(jnp.logical_not(listed))
            def _(rows=rows, at=at):
                panel[rows, at * B : (at + 1) * B] = jnp.zeros((B, B), jnp.bfloat16)


def sums_kernel(slots, struct_ref, a_ref, code_ref, *refs):
    outs, panel = refs[:-1], refs[-1]
    load_panel(code_ref, panel, struct_ref, slots)
    blocks = a_ref.shape[0] // B
    powers = [[] for _ in outs]
    for b in range(blocks):
        rows = slice(b * B, (b + 1) * B)
        total = -jnp.dot(a_ref[rows], panel[...], preferred_element_type=jnp.float32)
        for i, ref in enumerate(outs):
            part = total[:, i * B : (i + 1) * B]
            power = column_power(part)
            ref[rows] = to_code(part * (jnp.exp2(15.0 - power) * FILL))
            powers[i].append(power)
    for ref, power in zip(outs, powers):
        put_tail(ref, power, blocks * B)


def came_step(ref, blocks):
    return jnp.exp2(from_code(ref[blocks * B : blocks * B + TAIL]) - 15.0) * (1.0 / FILL)


def pair_kernel(to_two, own_ref, one_ref, out_ref):
    shard = own_ref.shape[0]
    for at, ref in enumerate((to_two, own_ref, one_ref)):
        out_ref[at * shard : (at + 1) * shard] = ref[...]


def base_kernel(came_ref, base_ref):
    blocks = base_ref.shape[0] // B
    step = came_step(came_ref, blocks)
    for b in range(blocks):
        rows = slice(b * B, (b + 1) * B)
        base_ref[rows] = from_code(came_ref[rows]) * step[b : b + 1]


def own_kernel(
    struct_ref, a_ref, pair, two, their_pair, their_two, base_ref, own_ref, panel
):
    p, z, c = place()
    shard = panel.shape[0] // 8
    for flip in range(4):
        for refs, core in (((pair, two), c), ((their_pair, their_two), 1 - c)):
            at = pl.multiple_of((2 * (z ^ flip) + core) * shard, FINE)
            part = slice((flip % 2) * shard, (flip % 2 + 1) * shard)
            panel[pl.ds(at, shard)] = refs[flip // 2][part]
    blocks = panel.shape[0] // B
    for block in range(blocks):

        @pl.when(jnp.logical_not(is_member(struct_ref, p, p * blocks + block)))
        def _(block=block):
            panel[block * B : (block + 1) * B] = jnp.zeros((B, B), jnp.bfloat16)

    own_ref[...] = base_ref[...] - jnp.dot(
        a_ref[...], panel[...], preferred_element_type=jnp.float32
    )


def route_kernel(own, x, y, both, *outs):
    p, z, _ = place()
    for flip, out in enumerate(outs):
        for turn, ref in enumerate((own, x, y, both)):

            @pl.when((p ^ z) == (turn ^ flip))
            def _(ref=ref, out=out):
                out[...] = ref[...]


def share_kernel(own, one, two, three, keep_ref, give_ref):
    _, z, c = place()
    shard = own.shape[0]
    for flip, ref in enumerate((own, one, two, three)):
        chip = z ^ flip
        at = pl.multiple_of((chip % 2) * shard, 64)

        @pl.when(chip // 2 == c)
        def _(ref=ref, at=at):
            keep_ref[pl.ds(at, shard)] = ref[:shard]

        @pl.when(chip // 2 != c)
        def _(ref=ref, at=at):
            give_ref[pl.ds(at, shard)] = ref[:shard]


def turn_kernel(keep, came, out_ref, lower):
    _, _, c = place()
    shard = keep.shape[0] // 2
    for half in range(2):
        for ref, core in ((keep, c), (came, 1 - c)):
            at = pl.multiple_of((2 * half + core) * shard, FINE)
            lower[pl.ds(at, shard)] = ref[half * shard : (half + 1) * shard]
    out_ref[...] = jnp.transpose(lower[...])


def last_kernel(
    struct_ref, own_ref, came_x, came_y, lower, off_ref, diag_ref, both
):
    p, z, c = place()
    blocks = off_ref.shape[0] // B
    first = (2 * z + c) * blocks
    steps = [came_step(ref, blocks) for ref in (came_x, came_y)]
    for b in range(blocks):
        rows = slice(b * B, (b + 1) * B)
        total = own_ref[rows]
        for ref, step in zip((came_x, came_y), steps):
            total = total + from_code(ref[rows]) * step[b : b + 1]
        total = jnp.where(is_member(struct_ref, p, first + b), total, 0.0)
        high = total.astype(jnp.bfloat16)
        off_ref[rows] = high
        both[rows, :B] = high
        both[rows, B:] = (total - high.astype(jnp.float32)).astype(jnp.bfloat16)
    diag = jnp.dot(lower[...], both[...], preferred_element_type=jnp.float32)
    diag = diag[:, :B] + diag[:, B:]
    piece = B // 8
    for zz in range(4):
        for cc in range(2):
            flip = zz ^ z
            core = jnp.where(flip == 1, 0, jnp.where(flip == 2, 1, cc))
            slot = jnp.where(flip == 0, 3, jnp.where(flip == 3, 2, cc)) + 4 * (core ^ c)
            at = (2 * zz + cc) * piece
            diag_ref[pl.ds(pl.multiple_of(slot * piece, piece), piece)] = diag[at : at + piece]


def send(value, move):
    found = []
    for p in range(4):
        for z in range(4):
            for c in range(2):
                to = move(p, z, c)
                found.append((p * 8 + 2 * z + c, to[0] * 8 + 2 * to[1] + to[2]))
    return lax.ppermute(value, AXES, found)


def chip_swap(p, z, c):
    return (p, z, 1 - c)


def along(flip):
    return lambda p, z, c: (p, z ^ flip, c)


def across(flip):
    return lambda p, z, c: (p ^ flip, z, c)


def after(value, *earlier):
    return lax.optimization_barrier((value, *earlier))[0]


def line_body(ancestor_inverse, lower_panel, pivot_inverse, struct_list):
    rows, depth = ancestor_inverse.shape
    shard = lower_panel.shape[0]
    bf16, f32, i16 = jnp.bfloat16, jnp.float32, jnp.int16
    shape = jax.ShapeDtypeStruct
    piece = shape((shard, B), bf16)
    code, keep, to_x, to_y, to_both = call(
        code_kernel,
        (shape((shard, 3 * B), i16),) + (piece,) * 4,
        [VM],
        [],
        8 * shard * NK * B,
        4 * shard * NK * B,
        "code",
    )(lower_panel)
    def small(kernel, outs, name, *args, flops=1):
        return call(kernel, outs, [VM] * len(args), [], flops, 1, name, room=2**21)(*args)

    own_piece = keep
    far_one = send(keep, along(1))
    rows_x = send(to_x, across(1))
    rows_y = send(to_y, across(2))
    rows_both = send(to_both, across(3))
    gathered = lax.all_gather(code, "pcol", axis=0, tiled=True)

    coded = shape((rows + TAIL, B), i16)

    def sums(slots, outs, name, *args):
        return call(
            functools.partial(sums_kernel, slots),
            (coded,) * outs,
            [SM, VM, VM],
            [pltpu.VMEM((depth, outs * B), bf16)],
            1,
            1,
            name,
        )(*args)

    (part_d,) = sums(((0, 3),), 1, "sums_d", struct_list, ancestor_inverse, gathered)
    came_d = send(part_d, across(3))
    part_x, part_y = sums(
        ((1, 1), (2, 2)), 2, "sums_xy", after(struct_list, part_d), ancestor_inverse, gathered
    )
    came_x = send(part_x, across(1))
    came_y = send(part_y, across(2))
    stay, to_one, to_two, to_three = small(
        route_kernel, (piece,) * 4, "route", keep, rows_x, rows_y, rows_both, flops=8 * 10**9
    )
    to_one, to_two, to_three, _ = lax.optimization_barrier((to_one, to_two, to_three, part_d))
    from_one = send(to_one, along(1))
    trio = small(
        pair_kernel, shape((3 * shard, B), bf16), "pair", to_two, own_piece, far_one, flops=3 * 10**9
    )
    from_two = send(trio, along(2))
    pair, two = trio[shard:], from_two[shard:]
    their_pair = send(pair, chip_swap)
    from_three = send(to_three, along(3))
    base = small(base_kernel, shape((rows, B), f32), "base", came_d, flops=4 * 10**9)
    own = call(
        own_kernel,
        shape((rows, B), f32),
        [SM] + [VM] * 6,
        [pltpu.VMEM((depth, B), bf16)],
        1,
        1,
        "own",
    )(struct_list, ancestor_inverse, pair, two, their_pair, send(two, chip_swap), base)
    half_rows = shape((2 * shard, B), bf16)
    keep, give = small(
        share_kernel, (half_rows, half_rows), "share", stay, from_one, from_two, from_three, flops=2 * 10**9
    )
    lower = call(
        turn_kernel,
        shape((B, rows), bf16),
        [VM, VM],
        [pltpu.VMEM((rows, B), bf16)],
        1,
        1,
        "turn",
    )(keep, send(give, chip_swap))
    off_inverse, diag = call(
        last_kernel,
        (shape((rows, B), bf16), shape((B, B), f32)),
        [SM] + [VM] * 4,
        [pltpu.VMEM((rows, 2 * B), bf16)],
        4 * rows * B * B,
        8 * rows * B,
        "last",
    )(struct_list, own, came_x, came_y, lower)

    half, part = B // 2, B // 8
    total = diag[:half] + send(diag[half:], chip_swap)
    pair = send(total[: 2 * part], lambda p, z, c: (p, z ^ (1 + c), c))
    total = total[3 * part :] + send(total[2 * part : 3 * part], along(3))
    even = lax.axis_index("pcol") % 2 == 0
    kept = jnp.where(even, pair[:part], pair[part:])
    other = send(jnp.where(even, pair[part:], pair[:part]), chip_swap)
    return off_inverse, pivot_inverse - (total + kept + other)


def body(ancestor_inverse, lower_panel, pivot_inverse, struct_list):
    rows, depth = ancestor_inverse.shape
    shard = lower_panel.shape[0]
    line = (
        lax.axis_size("prow") == 4
        and lax.axis_size("pcol") == 8
        and depth == 8 * shard
        and depth == 2 * rows
        and shard % 64 == 0
        and shard <= B
    )
    plan = line_body if line else general_body
    return plan(ancestor_inverse, lower_panel, pivot_inverse, struct_list)


def solution(mesh):
    placed = (P("pcol", "prow"), P(("prow", "pcol"), None), P("pcol", "prow"), P())
    return jax.shard_map(
        body,
        mesh=mesh,
        in_specs=placed,
        out_specs=(P("pcol", "prow"), P("pcol", "prow")),
        check_vma=False,
    )
```

```python
import functools

import jax
import jax.numpy as jnp
from jax import lax
from jax.experimental import pallas as pl
from jax.experimental.pallas import tpu as pltpu
from jax.sharding import PartitionSpec as P

B = 256
NK = 4
AXES = ("prow", "pcol")
TAIL = 16


def from_root(value, axis, root):
    mine = lax.axis_index(axis) == root
    return lax.psum(jnp.where(mine, value, jnp.zeros_like(value)), axis)


def membership(struct_list, ancestor_ids):
    listed = struct_list[:, :, None] == ancestor_ids[None, None, :]
    return jnp.transpose(jnp.any(listed, axis=1))


def general_body(ancestor_inverse, lower_panel, pivot_inverse, struct_list):
    row_count = ancestor_inverse.shape[0] // B
    col_count = ancestor_inverse.shape[1] // B
    grid_rows = lax.axis_size("prow")
    prow_index = lax.axis_index("prow")
    pcol_index = lax.axis_index("pcol")
    col_share = NK * B // grid_rows
    gathered = lax.all_gather(lower_panel, "pcol", axis=0, tiled=True)
    col_ids = prow_index * col_count + jnp.arange(col_count, dtype=jnp.int32)
    row_ids = pcol_index * row_count + jnp.arange(row_count, dtype=jnp.int32)
    member_cols = membership(struct_list, col_ids)
    member_rows = membership(struct_list, row_ids)
    scaled = gathered.reshape(col_count, B, NK, B) * member_cols[:, None, :, None].astype(
        jnp.bfloat16
    )
    masked = scaled.reshape(col_count * B, NK * B)
    partial_value = -jnp.dot(ancestor_inverse, masked, preferred_element_type=jnp.float32)
    share_sum = lax.psum_scatter(partial_value, "prow", scatter_dimension=1, tiled=True)
    columns = prow_index * col_share + jnp.arange(col_share, dtype=jnp.int32)
    block_of = columns // B
    one_hot = block_of[:, None] == jnp.arange(NK, dtype=jnp.int32)[None, :]
    row_mask = jnp.any(member_rows[:, None, :] & one_hot[None, :, :], axis=2).astype(jnp.float32)
    off_share = (share_sum.reshape(row_count, B, col_share) * row_mask[:, None, :]).reshape(
        row_count * B, col_share
    )
    off_inverse = off_share.astype(jnp.bfloat16)
    block_count = max(col_share // B, 1)
    column_width = col_share // block_count
    offset_blocks = pcol_index * row_count % col_count
    root_row = pcol_index * row_count // col_count
    piece = lax.dynamic_slice_in_dim(masked, offset_blocks * B, row_count * B, 0)
    lower_rows = from_root(piece, "prow", root_row)
    first_block = prow_index * col_share // B
    lower_slice = lax.dynamic_slice_in_dim(lower_rows, first_block * B, block_count * B, 1)
    lower_blocks = lower_slice.astype(jnp.float32).reshape(row_count * B, block_count, B)
    off_blocks = off_share.reshape(row_count * B, block_count, column_width)
    diag_term = jnp.einsum(
        "ikr,ikc->rkc", lower_blocks, off_blocks, precision=lax.Precision.HIGHEST
    ).reshape(B, col_share)
    diag_share = lax.psum_scatter(diag_term, "pcol", scatter_dimension=0, tiled=True)
    diag_inverse = pivot_inverse - diag_share
    return (off_inverse, diag_inverse)


VM = pl.BlockSpec(memory_space=pltpu.VMEM)
SM = pl.BlockSpec(memory_space=pltpu.SMEM)
FINE = 64
TINY = 2.0**-100
FILL = 0.9999


def place():
    p = lax.axis_index("prow")
    q = lax.axis_index("pcol")
    return p, q // 2, q % 2


def call(kernel, outs, specs, scratch, flops, moved, name, room=2**23):
    return pl.pallas_call(
        kernel,
        out_shape=outs,
        in_specs=specs,
        out_specs=jax.tree.map(lambda _: VM, outs),
        scratch_shapes=scratch,
        compiler_params=pltpu.CompilerParams(vmem_limit_bytes=room),
        cost_estimate=pl.CostEstimate(flops=flops, bytes_accessed=moved, transcendentals=0),
        name=name,
    )


def is_member(struct_ref, level, ancestor):
    found = struct_ref[level, 0] == ancestor
    for slot in range(1, struct_ref.shape[1]):
        found = found | (struct_ref[level, slot] == ancestor)
    return found


def column_power(value):
    top = jnp.maximum(jnp.max(jnp.abs(value), axis=0, keepdims=True), 2e-34)
    power = jnp.floor(jnp.log2(top)) + 1.0
    return jnp.where(top >= jnp.exp2(power), power + 1.0, power)


def put_tail(ref, powers, rows):
    row = lax.broadcasted_iota(jnp.int32, (TAIL, ref.shape[1]), 0)
    tail = jnp.zeros((TAIL, ref.shape[1]), jnp.float32)
    for block, power in enumerate(powers):
        tail = jnp.where(row == block, power, tail)
    ref[rows : rows + TAIL] = tail.astype(jnp.int32).astype(jnp.int16)


def to_code(value):
    return jnp.round(value).astype(jnp.int32).astype(jnp.int16)


def from_code(code):
    return code.astype(jnp.int32).astype(jnp.float32)


def code_kernel(lower_ref, code_ref, own, to_x, to_y, to_both):
    p, _, _ = place()

    def level(k):
        return lower_ref[:, pl.ds(pl.multiple_of(k * B, B), B)]

    for flip, out in enumerate((own, to_x, to_y, to_both)):
        out[...] = level(p ^ flip)
    for slot, flip in enumerate((3, 1, 2)):
        value = level(p ^ flip).astype(jnp.float32)
        size = jnp.abs(value)
        power = jnp.floor(jnp.log2(jnp.maximum(size, TINY)))
        code = jnp.round(size * jnp.exp2(7.0 - power)) + (power + 126.0) * 128.0
        code = jnp.where(size < TINY, 0.0, jnp.where(value < 0.0, -code, code))
        code_ref[:, slot * B : (slot + 1) * B] = code.astype(jnp.int32).astype(jnp.int16)


def load_panel(code_ref, panel, struct_ref, slots):
    p, _, _ = place()
    blocks = panel.shape[0] // B
    for at, (slot, flip) in enumerate(slots):
        for block in range(blocks):
            rows = slice(block * B, (block + 1) * B)
            listed = is_member(struct_ref, p ^ flip, p * blocks + block)

            @pl.when(listed)
            def _(rows=rows, at=at, slot=slot):
                code = code_ref[rows, slot * B : (slot + 1) * B].astype(jnp.int32)
                size = jnp.abs(code)
                power = jnp.exp2(((size >> 7) - 134).astype(jnp.float32))
                value = ((size & 127) + 128).astype(jnp.float32) * power
                panel[rows, at * B : (at + 1) * B] = jnp.where(code < 0, -value, value).astype(
                    jnp.bfloat16
                )

            @pl.when(jnp.logical_not(listed))
            def _(rows=rows, at=at):
                panel[rows, at * B : (at + 1) * B] = jnp.zeros((B, B), jnp.bfloat16)


def sums_kernel(slots, struct_ref, a_ref, code_ref, *refs):
    outs, panel = refs[:-1], refs[-1]
    load_panel(code_ref, panel, struct_ref, slots)
    blocks = a_ref.shape[0] // B
    powers = [[] for _ in outs]
    for b in range(blocks):
        rows = slice(b * B, (b + 1) * B)
        total = -jnp.dot(a_ref[rows], panel[...], preferred_element_type=jnp.float32)
        for i, ref in enumerate(outs):
            part = total[:, i * B : (i + 1) * B]
            power = column_power(part)
            ref[rows] = to_code(part * (jnp.exp2(15.0 - power) * FILL))
            powers[i].append(power)
    for ref, power in zip(outs, powers):
        put_tail(ref, power, blocks * B)


def came_step(ref, blocks):
    return jnp.exp2(from_code(ref[blocks * B : blocks * B + TAIL]) - 15.0) * (1.0 / FILL)


def pair_kernel(to_two, own_ref, one_ref, out_ref):
    shard = own_ref.shape[0]
    for at, ref in enumerate((to_two, own_ref, one_ref)):
        out_ref[at * shard : (at + 1) * shard] = ref[...]


def base_kernel(came_ref, near_ref, base_ref):
    blocks = base_ref.shape[0] // B
    step = came_step(came_ref, blocks)
    for b in range(blocks):
        rows = slice(b * B, (b + 1) * B)
        base_ref[rows] = near_ref[rows] + from_code(came_ref[rows]) * step[b : b + 1]


def own_kernel(far, struct_ref, a_ref, mine, theirs, *refs):
    own_ref, panel = refs[-2:]
    p, z, c = place()
    shard = mine.shape[0] // 2
    half = (z // 2) ^ far
    for i in range(2):
        chip = ((z ^ i) % 2) * 2
        for ref, core in ((mine, c), (theirs, 1 - c)):
            at = pl.multiple_of((chip + core) * shard, FINE)
            panel[pl.ds(at, shard)] = ref[i * shard : (i + 1) * shard]
    blocks = panel.shape[0] // B
    for block in range(blocks):
        listed = is_member(struct_ref, p, (2 * p + half) * blocks + block)

        @pl.when(jnp.logical_not(listed))
        def _(block=block):
            panel[block * B : (block + 1) * B] = jnp.zeros((B, B), jnp.bfloat16)

    depth = panel.shape[0]
    columns = a_ref[:, pl.ds(pl.multiple_of(half * depth, depth), depth)]
    total = -jnp.dot(columns, panel[...], preferred_element_type=jnp.float32)
    own_ref[...] = total + refs[0][...] if far else total


def route_kernel(own, x, y, both, *outs):
    p, z, _ = place()
    for flip, out in enumerate(outs):
        for turn, ref in enumerate((own, x, y, both)):

            @pl.when((p ^ z) == (turn ^ flip))
            def _(ref=ref, out=out):
                out[...] = ref[...]


def share_kernel(own, one, two, three, keep_ref, give_ref):
    _, z, c = place()
    shard = own.shape[0]
    for flip, ref in enumerate((own, one, two, three)):
        chip = z ^ flip
        at = pl.multiple_of((chip % 2) * shard, 64)

        @pl.when(chip // 2 == c)
        def _(ref=ref, at=at):
            keep_ref[pl.ds(at, shard)] = ref[:shard]

        @pl.when(chip // 2 != c)
        def _(ref=ref, at=at):
            give_ref[pl.ds(at, shard)] = ref[:shard]


def turn_kernel(keep, came, out_ref, lower):
    _, _, c = place()
    shard = keep.shape[0] // 2
    for half in range(2):
        for ref, core in ((keep, c), (came, 1 - c)):
            at = pl.multiple_of((2 * half + core) * shard, FINE)
            lower[pl.ds(at, shard)] = ref[half * shard : (half + 1) * shard]
    out_ref[...] = jnp.transpose(lower[...])


def last_kernel(
    struct_ref, own_ref, came_x, came_y, lower, off_ref, diag_ref, both
):
    p, z, c = place()
    blocks = off_ref.shape[0] // B
    first = (2 * z + c) * blocks
    steps = [came_step(ref, blocks) for ref in (came_x, came_y)]
    for b in range(blocks):
        rows = slice(b * B, (b + 1) * B)
        total = own_ref[rows]
        for ref, step in zip((came_x, came_y), steps):
            total = total + from_code(ref[rows]) * step[b : b + 1]
        total = jnp.where(is_member(struct_ref, p, first + b), total, 0.0)
        high = total.astype(jnp.bfloat16)
        off_ref[rows] = high
        both[rows, :B] = high
        both[rows, B:] = (total - high.astype(jnp.float32)).astype(jnp.bfloat16)
    diag = jnp.dot(lower[...], both[...], preferred_element_type=jnp.float32)
    diag = diag[:, :B] + diag[:, B:]
    piece = B // 8
    for zz in range(4):
        for cc in range(2):
            flip = zz ^ z
            core = jnp.where(flip == 1, 0, jnp.where(flip == 2, 1, cc))
            slot = jnp.where(flip == 0, 3, jnp.where(flip == 3, 2, cc)) + 4 * (core ^ c)
            at = (2 * zz + cc) * piece
            diag_ref[pl.ds(pl.multiple_of(slot * piece, piece), piece)] = diag[at : at + piece]


def send(value, move):
    found = []
    for p in range(4):
        for z in range(4):
            for c in range(2):
                to = move(p, z, c)
                found.append((p * 8 + 2 * z + c, to[0] * 8 + 2 * to[1] + to[2]))
    return lax.ppermute(value, AXES, found)


def chip_swap(p, z, c):
    return (p, z, 1 - c)


def along(flip):
    return lambda p, z, c: (p, z ^ flip, c)


def across(flip):
    return lambda p, z, c: (p ^ flip, z, c)


def after(value, *earlier):
    return lax.optimization_barrier((value, *earlier))[0]


def line_body(ancestor_inverse, lower_panel, pivot_inverse, struct_list):
    rows, depth = ancestor_inverse.shape
    shard = lower_panel.shape[0]
    bf16, f32, i16 = jnp.bfloat16, jnp.float32, jnp.int16
    shape = jax.ShapeDtypeStruct
    piece = shape((shard, B), bf16)
    code, keep, to_x, to_y, to_both = call(
        code_kernel,
        (shape((shard, 3 * B), i16),) + (piece,) * 4,
        [VM],
        [],
        8 * shard * NK * B,
        4 * shard * NK * B,
        "code",
    )(lower_panel)
    def small(kernel, outs, name, *args, flops=1):
        return call(kernel, outs, [VM] * len(args), [], flops, 1, name, room=2**21)(*args)

    own_piece = keep
    far_one = send(keep, along(1))
    rows_x = send(to_x, across(1))
    rows_y = send(to_y, across(2))
    rows_both = send(to_both, across(3))
    gathered = lax.all_gather(code, "pcol", axis=0, tiled=True)

    coded = shape((rows + TAIL, B), i16)

    def sums(slots, outs, name, *args):
        return call(
            functools.partial(sums_kernel, slots),
            (coded,) * outs,
            [SM, VM, VM],
            [pltpu.VMEM((depth, outs * B), bf16)],
            1,
            1,
            name,
        )(*args)

    (part_d,) = sums(((0, 3),), 1, "sums_d", struct_list, ancestor_inverse, gathered)
    came_d = send(part_d, across(3))
    part_x, part_y = sums(
        ((1, 1), (2, 2)), 2, "sums_xy", after(struct_list, part_d), ancestor_inverse, gathered
    )
    came_x = send(part_x, across(1))
    stay, to_one, to_two, to_three = small(
        route_kernel, (piece,) * 4, "route", keep, rows_x, rows_y, rows_both, flops=8 * 10**9
    )
    to_one, to_two, to_three, _ = lax.optimization_barrier((to_one, to_two, to_three, part_d))
    from_one = send(to_one, along(1))
    trio = small(
        pair_kernel, shape((3 * shard, B), bf16), "pair", to_two, own_piece, far_one, flops=3 * 10**9
    )
    from_two = send(trio, along(2))
    pair, two = trio[shard:], from_two[shard:]
    their_pair = send(pair, chip_swap)
    def own_half(far, *args, flops=1):
        return call(
            functools.partial(own_kernel, far),
            shape((rows, B), f32),
            [SM] + [VM] * (1 + len(args)),
            [pltpu.VMEM((depth // 2, B), bf16)],
            flops,
            1,
            "own",
        )(struct_list, ancestor_inverse, *args)

    near_own = own_half(0, pair, their_pair)
    came_y = send(after(part_y, near_own), across(2))
    from_three = send(to_three, along(3))
    base = small(base_kernel, shape((rows, B), f32), "base", came_d, near_own, flops=4 * 10**9)
    own = own_half(1, two, send(two, chip_swap), base)
    half_rows = shape((2 * shard, B), bf16)
    keep, give = small(
        share_kernel, (half_rows, half_rows), "share", stay, from_one, from_two, from_three, flops=2 * 10**9
    )
    lower = call(
        turn_kernel,
        shape((B, rows), bf16),
        [VM, VM],
        [pltpu.VMEM((rows, B), bf16)],
        1,
        1,
        "turn",
    )(keep, send(give, chip_swap))
    off_inverse, diag = call(
        last_kernel,
        (shape((rows, B), bf16), shape((B, B), f32)),
        [SM] + [VM] * 4,
        [pltpu.VMEM((rows, 2 * B), bf16)],
        4 * rows * B * B,
        8 * rows * B,
        "last",
    )(struct_list, own, came_x, came_y, lower)

    half, part = B // 2, B // 8
    total = diag[:half] + send(diag[half:], chip_swap)
    pair = send(total[: 2 * part], lambda p, z, c: (p, z ^ (1 + c), c))
    total = total[3 * part :] + send(total[2 * part : 3 * part], along(3))
    even = lax.axis_index("pcol") % 2 == 0
    kept = jnp.where(even, pair[:part], pair[part:])
    other = send(jnp.where(even, pair[part:], pair[:part]), chip_swap)
    return off_inverse, pivot_inverse - (total + kept + other)


def body(ancestor_inverse, lower_panel, pivot_inverse, struct_list):
    rows, depth = ancestor_inverse.shape
    shard = lower_panel.shape[0]
    line = (
        lax.axis_size("prow") == 4
        and lax.axis_size("pcol") == 8
        and depth == 8 * shard
        and depth == 2 * rows
        and shard % 64 == 0
        and shard <= B
    )
    plan = line_body if line else general_body
    return plan(ancestor_inverse, lower_panel, pivot_inverse, struct_list)


def solution(mesh):
    placed = (P("pcol", "prow"), P(("prow", "pcol"), None), P("pcol", "prow"), P())
    return jax.shard_map(
        body,
        mesh=mesh,
        in_specs=placed,
        out_specs=(P("pcol", "prow"), P("pcol", "prow")),
        check_vma=False,
    )
```

```python
import functools

import jax
import jax.numpy as jnp
from jax import lax
from jax.experimental import pallas as pl
from jax.experimental.pallas import tpu as pltpu
from jax.sharding import PartitionSpec as P

B = 256
NK = 4
AXES = ("prow", "pcol")
TAIL = 16


def from_root(value, axis, root):
    mine = lax.axis_index(axis) == root
    return lax.psum(jnp.where(mine, value, jnp.zeros_like(value)), axis)


def membership(struct_list, ancestor_ids):
    listed = struct_list[:, :, None] == ancestor_ids[None, None, :]
    return jnp.transpose(jnp.any(listed, axis=1))


def general_body(ancestor_inverse, lower_panel, pivot_inverse, struct_list):
    row_count = ancestor_inverse.shape[0] // B
    col_count = ancestor_inverse.shape[1] // B
    grid_rows = lax.axis_size("prow")
    prow_index = lax.axis_index("prow")
    pcol_index = lax.axis_index("pcol")
    col_share = NK * B // grid_rows
    gathered = lax.all_gather(lower_panel, "pcol", axis=0, tiled=True)
    col_ids = prow_index * col_count + jnp.arange(col_count, dtype=jnp.int32)
    row_ids = pcol_index * row_count + jnp.arange(row_count, dtype=jnp.int32)
    member_cols = membership(struct_list, col_ids)
    member_rows = membership(struct_list, row_ids)
    scaled = gathered.reshape(col_count, B, NK, B) * member_cols[:, None, :, None].astype(
        jnp.bfloat16
    )
    masked = scaled.reshape(col_count * B, NK * B)
    partial_value = -jnp.dot(ancestor_inverse, masked, preferred_element_type=jnp.float32)
    share_sum = lax.psum_scatter(partial_value, "prow", scatter_dimension=1, tiled=True)
    columns = prow_index * col_share + jnp.arange(col_share, dtype=jnp.int32)
    block_of = columns // B
    one_hot = block_of[:, None] == jnp.arange(NK, dtype=jnp.int32)[None, :]
    row_mask = jnp.any(member_rows[:, None, :] & one_hot[None, :, :], axis=2).astype(jnp.float32)
    off_share = (share_sum.reshape(row_count, B, col_share) * row_mask[:, None, :]).reshape(
        row_count * B, col_share
    )
    off_inverse = off_share.astype(jnp.bfloat16)
    block_count = max(col_share // B, 1)
    column_width = col_share // block_count
    offset_blocks = pcol_index * row_count % col_count
    root_row = pcol_index * row_count // col_count
    piece = lax.dynamic_slice_in_dim(masked, offset_blocks * B, row_count * B, 0)
    lower_rows = from_root(piece, "prow", root_row)
    first_block = prow_index * col_share // B
    lower_slice = lax.dynamic_slice_in_dim(lower_rows, first_block * B, block_count * B, 1)
    lower_blocks = lower_slice.astype(jnp.float32).reshape(row_count * B, block_count, B)
    off_blocks = off_share.reshape(row_count * B, block_count, column_width)
    diag_term = jnp.einsum(
        "ikr,ikc->rkc", lower_blocks, off_blocks, precision=lax.Precision.HIGHEST
    ).reshape(B, col_share)
    diag_share = lax.psum_scatter(diag_term, "pcol", scatter_dimension=0, tiled=True)
    diag_inverse = pivot_inverse - diag_share
    return (off_inverse, diag_inverse)


VM = pl.BlockSpec(memory_space=pltpu.VMEM)
SM = pl.BlockSpec(memory_space=pltpu.SMEM)
FINE = 64
TINY = 2.0**-100
FILL = 0.9999


def place():
    p = lax.axis_index("prow")
    q = lax.axis_index("pcol")
    return p, q // 2, q % 2


def call(kernel, outs, specs, scratch, flops, moved, name, room=2**23):
    return pl.pallas_call(
        kernel,
        out_shape=outs,
        in_specs=specs,
        out_specs=jax.tree.map(lambda _: VM, outs),
        scratch_shapes=scratch,
        compiler_params=pltpu.CompilerParams(vmem_limit_bytes=room),
        cost_estimate=pl.CostEstimate(flops=flops, bytes_accessed=moved, transcendentals=0),
        name=name,
    )


def is_member(struct_ref, level, ancestor):
    found = struct_ref[level, 0] == ancestor
    for slot in range(1, struct_ref.shape[1]):
        found = found | (struct_ref[level, slot] == ancestor)
    return found


def put_tail(ref, powers, rows):
    row = lax.broadcasted_iota(jnp.int32, (TAIL, ref.shape[1]), 0)
    tail = jnp.zeros((TAIL, ref.shape[1]), jnp.float32)
    for block, power in enumerate(powers):
        tail = jnp.where(row == block, power, tail)
    ref[rows : rows + TAIL] = tail.astype(jnp.int32).astype(jnp.int16)


def to_code(value):
    return jnp.round(value).astype(jnp.int32).astype(jnp.int16)


def from_code(code):
    return code.astype(jnp.int32).astype(jnp.float32)


def code_kernel(lower_ref, code_ref, own, to_x, to_y, to_both):
    p, _, _ = place()

    def level(k):
        return lower_ref[:, pl.ds(pl.multiple_of(k * B, B), B)]

    for flip, out in enumerate((own, to_x, to_y, to_both)):
        out[...] = level(p ^ flip)
    for slot, flip in enumerate((3, 1, 2)):
        value = level(p ^ flip).astype(jnp.float32)
        size = jnp.abs(value)
        power = jnp.floor(jnp.log2(jnp.maximum(size, TINY)))
        code = jnp.round(size * jnp.exp2(7.0 - power)) + (power + 126.0) * 128.0
        code = jnp.where(size < TINY, 0.0, jnp.where(value < 0.0, -code, code))
        code_ref[:, slot * B : (slot + 1) * B] = code.astype(jnp.int32).astype(jnp.int16)


def load_panel(code_ref, panel, struct_ref, slots):
    p, _, _ = place()
    blocks = panel.shape[0] // B
    for at, (slot, flip) in enumerate(slots):
        for block in range(blocks):
            rows = slice(block * B, (block + 1) * B)
            listed = is_member(struct_ref, p ^ flip, p * blocks + block)

            @pl.when(listed)
            def _(rows=rows, at=at, slot=slot):
                code = code_ref[rows, slot * B : (slot + 1) * B].astype(jnp.int32)
                size = jnp.abs(code)
                power = jnp.exp2(((size >> 7) - 134).astype(jnp.float32))
                value = ((size & 127) + 128).astype(jnp.float32) * power
                panel[rows, at * B : (at + 1) * B] = jnp.where(code < 0, -value, value).astype(
                    jnp.bfloat16
                )

            @pl.when(jnp.logical_not(listed))
            def _(rows=rows, at=at):
                panel[rows, at * B : (at + 1) * B] = jnp.zeros((B, B), jnp.bfloat16)


def sums_kernel(slots, struct_ref, a_ref, code_ref, *refs):
    outs, panel = refs[:-1], refs[-1]
    load_panel(code_ref, panel, struct_ref, slots)
    blocks = a_ref.shape[0] // B
    powers = [[] for _ in outs]
    for b in range(blocks):
        rows = slice(b * B, (b + 1) * B)
        total = -jnp.dot(a_ref[rows], panel[...], preferred_element_type=jnp.float32)
        for i, ref in enumerate(outs):
            part = total[:, i * B : (i + 1) * B]
            top = jnp.maximum(jnp.max(jnp.abs(part), axis=0, keepdims=True), 2e-34)
            power = jnp.floor(jnp.log2(top)) + 1.0
            ref[rows] = to_code(part * (jnp.exp2(15.0 - power) * FILL))
            powers[i].append(power)
    for ref, power in zip(outs, powers):
        put_tail(ref, power, blocks * B)


def came_step(ref, blocks):
    return jnp.exp2(from_code(ref[blocks * B : blocks * B + TAIL]) - 15.0) * (1.0 / FILL)


def pair_kernel(to_two, own_ref, one_ref, out_ref):
    shard = own_ref.shape[0]
    for at, ref in enumerate((to_two, own_ref, one_ref)):
        out_ref[at * shard : (at + 1) * shard] = ref[...]


def base_kernel(came_ref, near_ref, base_ref):
    blocks = base_ref.shape[0] // B
    step = came_step(came_ref, blocks)
    for b in range(blocks):
        rows = slice(b * B, (b + 1) * B)
        base_ref[rows] = near_ref[rows] + from_code(came_ref[rows]) * step[b : b + 1]


def own_kernel(far, struct_ref, a_ref, mine, theirs, *refs):
    own_ref, panel = refs[-2:]
    p, z, c = place()
    shard = mine.shape[0] // 2
    half = (z // 2) ^ far
    for i in range(2):
        chip = ((z ^ i) % 2) * 2
        for ref, core in ((mine, c), (theirs, 1 - c)):
            at = pl.multiple_of((chip + core) * shard, FINE)
            panel[pl.ds(at, shard)] = ref[i * shard : (i + 1) * shard]
    blocks = panel.shape[0] // B
    for block in range(blocks):
        listed = is_member(struct_ref, p, (2 * p + half) * blocks + block)

        @pl.when(jnp.logical_not(listed))
        def _(block=block):
            panel[block * B : (block + 1) * B] = jnp.zeros((B, B), jnp.bfloat16)

    depth = panel.shape[0]
    columns = a_ref[:, pl.ds(pl.multiple_of(half * depth, depth), depth)]
    total = -jnp.dot(columns, panel[...], preferred_element_type=jnp.float32)
    own_ref[...] = total + refs[0][...] if far else total


def route_kernel(own, x, y, both, *outs):
    p, z, _ = place()
    for flip, out in enumerate(outs):
        for turn, ref in enumerate((own, x, y, both)):

            @pl.when((p ^ z) == (turn ^ flip))
            def _(ref=ref, out=out):
                out[...] = ref[...]


def share_kernel(own, one, two, three, keep_ref, give_ref):
    _, z, c = place()
    shard = own.shape[0]
    for flip, ref in enumerate((own, one, two, three)):
        chip = z ^ flip
        at = pl.multiple_of((chip % 2) * shard, 64)

        @pl.when(chip // 2 == c)
        def _(ref=ref, at=at):
            keep_ref[pl.ds(at, shard)] = ref[:shard]

        @pl.when(chip // 2 != c)
        def _(ref=ref, at=at):
            give_ref[pl.ds(at, shard)] = ref[:shard]


def turn_kernel(keep, came, out_ref, lower):
    _, _, c = place()
    shard = keep.shape[0] // 2
    for half in range(2):
        for ref, core in ((keep, c), (came, 1 - c)):
            at = pl.multiple_of((2 * half + core) * shard, FINE)
            lower[pl.ds(at, shard)] = ref[half * shard : (half + 1) * shard]
    out_ref[...] = jnp.transpose(lower[...])


def last_kernel(
    struct_ref, own_ref, came_x, came_y, lower, off_ref, diag_ref, both
):
    p, z, c = place()
    blocks = off_ref.shape[0] // B
    first = (2 * z + c) * blocks
    steps = [came_step(ref, blocks) for ref in (came_x, came_y)]
    for b in range(blocks):
        rows = slice(b * B, (b + 1) * B)
        total = own_ref[rows]
        for ref, step in zip((came_x, came_y), steps):
            total = total + from_code(ref[rows]) * step[b : b + 1]
        total = jnp.where(is_member(struct_ref, p, first + b), total, 0.0)
        high = total.astype(jnp.bfloat16)
        off_ref[rows] = high
        both[rows, :B] = high
        both[rows, B:] = (total - high.astype(jnp.float32)).astype(jnp.bfloat16)
    diag = jnp.dot(lower[...], both[...], preferred_element_type=jnp.float32)
    diag = diag[:, :B] + diag[:, B:]
    piece = B // 8
    for zz in range(4):
        for cc in range(2):
            flip = zz ^ z
            core = jnp.where(flip == 1, 0, jnp.where(flip == 2, 1, cc))
            slot = jnp.where(flip == 0, 3, jnp.where(flip == 3, 2, cc)) + 4 * (core ^ c)
            at = (2 * zz + cc) * piece
            diag_ref[pl.ds(pl.multiple_of(slot * piece, piece), piece)] = diag[at : at + piece]


def send(value, move):
    found = []
    for p in range(4):
        for z in range(4):
            for c in range(2):
                to = move(p, z, c)
                found.append((p * 8 + 2 * z + c, to[0] * 8 + 2 * to[1] + to[2]))
    return lax.ppermute(value, AXES, found)


def chip_swap(p, z, c):
    return (p, z, 1 - c)


def along(flip):
    return lambda p, z, c: (p, z ^ flip, c)


def across(flip):
    return lambda p, z, c: (p ^ flip, z, c)


def after(value, *earlier):
    return lax.optimization_barrier((value, *earlier))[0]


def line_body(ancestor_inverse, lower_panel, pivot_inverse, struct_list):
    rows, depth = ancestor_inverse.shape
    shard = lower_panel.shape[0]
    bf16, f32, i16 = jnp.bfloat16, jnp.float32, jnp.int16
    shape = jax.ShapeDtypeStruct
    piece = shape((shard, B), bf16)
    code, keep, to_x, to_y, to_both = call(
        code_kernel,
        (shape((shard, 3 * B), i16),) + (piece,) * 4,
        [VM],
        [],
        8 * shard * NK * B,
        4 * shard * NK * B,
        "code",
    )(lower_panel)
    def small(kernel, outs, name, *args, flops=1):
        return call(kernel, outs, [VM] * len(args), [], flops, 1, name, room=2**21)(*args)

    own_piece = keep
    far_one = send(keep, along(1))
    rows_x = send(to_x, across(1))
    rows_y = send(to_y, across(2))
    rows_both = send(to_both, across(3))
    gathered = lax.all_gather(code, "pcol", axis=0, tiled=True)

    coded = shape((rows + TAIL, B), i16)

    def sums(slots, outs, name, *args):
        return call(
            functools.partial(sums_kernel, slots),
            (coded,) * outs,
            [SM, VM, VM],
            [pltpu.VMEM((depth, outs * B), bf16)],
            1,
            1,
            name,
        )(*args)

    (part_d,) = sums(((0, 3),), 1, "sums_d", struct_list, ancestor_inverse, gathered)
    came_d = send(part_d, across(3))
    part_x, part_y = sums(
        ((1, 1), (2, 2)), 2, "sums_xy", after(struct_list, part_d), ancestor_inverse, gathered
    )
    came_x = send(part_x, across(1))
    stay, to_one, to_two, to_three = small(
        route_kernel, (piece,) * 4, "route", keep, rows_x, rows_y, rows_both, flops=8 * 10**9
    )
    to_one, to_two, to_three, _ = lax.optimization_barrier((to_one, to_two, to_three, part_d))
    from_one = send(to_one, along(1))
    trio = small(
        pair_kernel, shape((3 * shard, B), bf16), "pair", to_two, own_piece, far_one, flops=3 * 10**9
    )
    from_two = send(trio, along(2))
    pair, two = trio[shard:], from_two[shard:]
    their_pair = send(pair, chip_swap)
    def own_half(far, *args, flops=1):
        return call(
            functools.partial(own_kernel, far),
            shape((rows, B), f32),
            [SM] + [VM] * (1 + len(args)),
            [pltpu.VMEM((depth // 2, B), bf16)],
            flops,
            1,
            "own",
        )(struct_list, ancestor_inverse, *args)

    near_own = own_half(0, pair, their_pair)
    came_y = send(after(part_y, near_own), across(2))
    from_three = send(to_three, along(3))
    base = small(base_kernel, shape((rows, B), f32), "base", came_d, near_own, flops=4 * 10**9)
    own = own_half(1, two, send(two, chip_swap), base)
    half_rows = shape((2 * shard, B), bf16)
    keep, give = small(
        share_kernel, (half_rows, half_rows), "share", stay, from_one, from_two, from_three, flops=2 * 10**9
    )
    lower = call(
        turn_kernel,
        shape((B, rows), bf16),
        [VM, VM],
        [pltpu.VMEM((rows, B), bf16)],
        1,
        1,
        "turn",
    )(keep, send(give, chip_swap))
    off_inverse, diag = call(
        last_kernel,
        (shape((rows, B), bf16), shape((B, B), f32)),
        [SM] + [VM] * 4,
        [pltpu.VMEM((rows, 2 * B), bf16)],
        4 * rows * B * B,
        8 * rows * B,
        "last",
    )(struct_list, own, came_x, came_y, lower)

    half, part = B // 2, B // 8
    total = diag[:half] + send(diag[half:], chip_swap)
    pair = send(total[: 2 * part], lambda p, z, c: (p, z ^ (1 + c), c))
    total = total[3 * part :] + send(total[2 * part : 3 * part], along(3))
    even = lax.axis_index("pcol") % 2 == 0
    kept = jnp.where(even, pair[:part], pair[part:])
    other = send(jnp.where(even, pair[part:], pair[:part]), chip_swap)
    return off_inverse, pivot_inverse - (total + kept + other)


def body(ancestor_inverse, lower_panel, pivot_inverse, struct_list):
    rows, depth = ancestor_inverse.shape
    shard = lower_panel.shape[0]
    line = (
        lax.axis_size("prow") == 4
        and lax.axis_size("pcol") == 8
        and depth == 8 * shard
        and depth == 2 * rows
        and shard % 64 == 0
        and shard <= B
    )
    plan = line_body if line else general_body
    return plan(ancestor_inverse, lower_panel, pivot_inverse, struct_list)


def solution(mesh):
    placed = (P("pcol", "prow"), P(("prow", "pcol"), None), P("pcol", "prow"), P())
    return jax.shard_map(
        body,
        mesh=mesh,
        in_specs=placed,
        out_specs=(P("pcol", "prow"), P("pcol", "prow")),
        check_vma=False,
    )
```

```python
import functools

import jax
import jax.numpy as jnp
from jax import lax
from jax.experimental import pallas as pl
from jax.experimental.pallas import tpu as pltpu
from jax.sharding import PartitionSpec as P

B = 256
NK = 4
AXES = ("prow", "pcol")
TAIL = 16


def from_root(value, axis, root):
    mine = lax.axis_index(axis) == root
    return lax.psum(jnp.where(mine, value, jnp.zeros_like(value)), axis)


def membership(struct_list, ancestor_ids):
    listed = struct_list[:, :, None] == ancestor_ids[None, None, :]
    return jnp.transpose(jnp.any(listed, axis=1))


def general_body(ancestor_inverse, lower_panel, pivot_inverse, struct_list):
    row_count = ancestor_inverse.shape[0] // B
    col_count = ancestor_inverse.shape[1] // B
    grid_rows = lax.axis_size("prow")
    prow_index = lax.axis_index("prow")
    pcol_index = lax.axis_index("pcol")
    col_share = NK * B // grid_rows
    gathered = lax.all_gather(lower_panel, "pcol", axis=0, tiled=True)
    col_ids = prow_index * col_count + jnp.arange(col_count, dtype=jnp.int32)
    row_ids = pcol_index * row_count + jnp.arange(row_count, dtype=jnp.int32)
    member_cols = membership(struct_list, col_ids)
    member_rows = membership(struct_list, row_ids)
    scaled = gathered.reshape(col_count, B, NK, B) * member_cols[:, None, :, None].astype(
        jnp.bfloat16
    )
    masked = scaled.reshape(col_count * B, NK * B)
    partial_value = -jnp.dot(ancestor_inverse, masked, preferred_element_type=jnp.float32)
    share_sum = lax.psum_scatter(partial_value, "prow", scatter_dimension=1, tiled=True)
    columns = prow_index * col_share + jnp.arange(col_share, dtype=jnp.int32)
    block_of = columns // B
    one_hot = block_of[:, None] == jnp.arange(NK, dtype=jnp.int32)[None, :]
    row_mask = jnp.any(member_rows[:, None, :] & one_hot[None, :, :], axis=2).astype(jnp.float32)
    off_share = (share_sum.reshape(row_count, B, col_share) * row_mask[:, None, :]).reshape(
        row_count * B, col_share
    )
    off_inverse = off_share.astype(jnp.bfloat16)
    block_count = max(col_share // B, 1)
    column_width = col_share // block_count
    offset_blocks = pcol_index * row_count % col_count
    root_row = pcol_index * row_count // col_count
    piece = lax.dynamic_slice_in_dim(masked, offset_blocks * B, row_count * B, 0)
    lower_rows = from_root(piece, "prow", root_row)
    first_block = prow_index * col_share // B
    lower_slice = lax.dynamic_slice_in_dim(lower_rows, first_block * B, block_count * B, 1)
    lower_blocks = lower_slice.astype(jnp.float32).reshape(row_count * B, block_count, B)
    off_blocks = off_share.reshape(row_count * B, block_count, column_width)
    diag_term = jnp.einsum(
        "ikr,ikc->rkc", lower_blocks, off_blocks, precision=lax.Precision.HIGHEST
    ).reshape(B, col_share)
    diag_share = lax.psum_scatter(diag_term, "pcol", scatter_dimension=0, tiled=True)
    diag_inverse = pivot_inverse - diag_share
    return (off_inverse, diag_inverse)


VM = pl.BlockSpec(memory_space=pltpu.VMEM)
SM = pl.BlockSpec(memory_space=pltpu.SMEM)
FINE = 64
TINY = 2.0**-100
FILL = 0.9999


def place():
    p = lax.axis_index("prow")
    q = lax.axis_index("pcol")
    return p, q // 2, q % 2


def call(kernel, outs, specs, scratch, flops, moved, name, room=2**23):
    return pl.pallas_call(
        kernel,
        out_shape=outs,
        in_specs=specs,
        out_specs=jax.tree.map(lambda _: VM, outs),
        scratch_shapes=scratch,
        compiler_params=pltpu.CompilerParams(vmem_limit_bytes=room),
        cost_estimate=pl.CostEstimate(flops=flops, bytes_accessed=moved, transcendentals=0),
        name=name,
    )


def is_member(struct_ref, level, ancestor):
    found = struct_ref[level, 0] == ancestor
    for slot in range(1, struct_ref.shape[1]):
        found = found | (struct_ref[level, slot] == ancestor)
    return found


def column_power(value):
    top = jnp.maximum(jnp.max(jnp.abs(value), axis=0, keepdims=True), 2e-34)
    power = jnp.floor(jnp.log2(top)) + 1.0
    return jnp.where(top >= jnp.exp2(power), power + 1.0, power)


def put_tail(ref, powers, rows):
    row = lax.broadcasted_iota(jnp.int32, (TAIL, ref.shape[1]), 0)
    tail = jnp.zeros((TAIL, ref.shape[1]), jnp.float32)
    for block, power in enumerate(powers):
        tail = jnp.where(row == block, power, tail)
    ref[rows : rows + TAIL] = tail.astype(jnp.int32).astype(jnp.int16)


def to_code(value):
    return jnp.round(value).astype(jnp.int32).astype(jnp.int16)


def from_code(code):
    return code.astype(jnp.int32).astype(jnp.float32)


def code_kernel(lower_ref, code_ref, own, to_x, to_y, to_both):
    p, _, _ = place()

    def level(k):
        return lower_ref[:, pl.ds(pl.multiple_of(k * B, B), B)]

    for flip, out in enumerate((own, to_x, to_y, to_both)):
        out[...] = level(p ^ flip)
    for slot, flip in enumerate((3, 1, 2)):
        value = level(p ^ flip).astype(jnp.float32)
        size = jnp.abs(value)
        power = jnp.floor(jnp.log2(jnp.maximum(size, TINY)))
        code = jnp.round(size * jnp.exp2(7.0 - power)) + (power + 126.0) * 128.0
        code = jnp.where(size < TINY, 0.0, jnp.where(value < 0.0, -code, code))
        code_ref[:, slot * B : (slot + 1) * B] = code.astype(jnp.int32).astype(jnp.int16)


def load_panel(code_ref, panel, struct_ref, slots):
    p, _, _ = place()
    blocks = panel.shape[0] // B
    for at, (slot, flip) in enumerate(slots):
        for block in range(blocks):
            rows = slice(block * B, (block + 1) * B)
            listed = is_member(struct_ref, p ^ flip, p * blocks + block)

            @pl.when(listed)
            def _(rows=rows, at=at, slot=slot):
                code = code_ref[rows, slot * B : (slot + 1) * B].astype(jnp.int32)
                size = jnp.abs(code)
                power = jnp.exp2(((size >> 7) - 134).astype(jnp.float32))
                value = ((size & 127) + 128).astype(jnp.float32) * power
                panel[rows, at * B : (at + 1) * B] = jnp.where(code < 0, -value, value).astype(
                    jnp.bfloat16
                )

            @pl.when(jnp.logical_not(listed))
            def _(rows=rows, at=at):
                panel[rows, at * B : (at + 1) * B] = jnp.zeros((B, B), jnp.bfloat16)


def sums_kernel(slots, struct_ref, a_ref, code_ref, *refs):
    outs, panel = refs[:-1], refs[-1]
    load_panel(code_ref, panel, struct_ref, slots)
    blocks = a_ref.shape[0] // B
    powers = [[] for _ in outs]
    for b in range(blocks):
        rows = slice(b * B, (b + 1) * B)
        total = -jnp.dot(a_ref[rows], panel[...], preferred_element_type=jnp.float32)
        for i, ref in enumerate(outs):
            part = total[:, i * B : (i + 1) * B]
            power = column_power(part)
            ref[rows] = to_code(part * (jnp.exp2(15.0 - power) * FILL))
            powers[i].append(power)
    for ref, power in zip(outs, powers):
        put_tail(ref, power, blocks * B)


def came_step(ref, blocks):
    return jnp.exp2(from_code(ref[blocks * B : blocks * B + TAIL]) - 15.0) * (1.0 / FILL)


def pair_kernel(to_two, own_ref, one_ref, out_ref):
    shard = own_ref.shape[0]
    for at, ref in enumerate((to_two, own_ref, one_ref)):
        out_ref[at * shard : (at + 1) * shard] = ref[...]


def base_kernel(came_ref, near_ref, base_ref):
    blocks = base_ref.shape[0] // B
    step = came_step(came_ref, blocks)
    for b in range(blocks):
        rows = slice(b * B, (b + 1) * B)
        base_ref[rows] = near_ref[rows] + from_code(came_ref[rows]) * step[b : b + 1]


def own_kernel(far, struct_ref, a_ref, mine, theirs, *refs):
    own_ref, panel = refs[-2:]
    p, z, c = place()
    shard = mine.shape[0] // 2
    half = (z // 2) ^ far
    for i in range(2):
        chip = ((z ^ i) % 2) * 2
        for ref, core in ((mine, c), (theirs, 1 - c)):
            at = pl.multiple_of((chip + core) * shard, FINE)
            panel[pl.ds(at, shard)] = ref[i * shard : (i + 1) * shard]
    blocks = panel.shape[0] // B
    for block in range(blocks):
        listed = is_member(struct_ref, p, (2 * p + half) * blocks + block)

        @pl.when(jnp.logical_not(listed))
        def _(block=block):
            panel[block * B : (block + 1) * B] = jnp.zeros((B, B), jnp.bfloat16)

    depth = panel.shape[0]
    columns = a_ref[:, pl.ds(pl.multiple_of(half * depth, depth), depth)]
    total = -jnp.dot(columns, panel[...], preferred_element_type=jnp.float32)
    own_ref[...] = total + refs[0][...] if far else total


def route_kernel(own, x, y, both, *outs):
    p, z, _ = place()
    for flip, out in enumerate(outs):
        for turn, ref in enumerate((own, x, y, both)):

            @pl.when((p ^ z) == (turn ^ flip))
            def _(ref=ref, out=out):
                out[...] = ref[...]


def share_kernel(own, one, two, three, keep_ref, give_ref):
    _, z, c = place()
    shard = own.shape[0]
    for flip, ref in enumerate((own, one, two, three)):
        chip = z ^ flip
        at = pl.multiple_of((chip % 2) * shard, 64)

        @pl.when(chip // 2 == c)
        def _(ref=ref, at=at):
            keep_ref[pl.ds(at, shard)] = ref[:shard]

        @pl.when(chip // 2 != c)
        def _(ref=ref, at=at):
            give_ref[pl.ds(at, shard)] = ref[:shard]


def turn_kernel(keep, came, out_ref, lower):
    _, _, c = place()
    shard = keep.shape[0] // 2
    for half in range(2):
        for ref, core in ((keep, c), (came, 1 - c)):
            at = pl.multiple_of((2 * half + core) * shard, FINE)
            lower[pl.ds(at, shard)] = ref[half * shard : (half + 1) * shard]
    out_ref[...] = jnp.transpose(lower[...])


def last_kernel(
    struct_ref, own_ref, came_x, came_y, lower, off_ref, diag_ref, both
):
    p, z, c = place()
    blocks = off_ref.shape[0] // B
    first = (2 * z + c) * blocks
    steps = [came_step(ref, blocks) for ref in (came_x, came_y)]
    for b in range(blocks):
        rows = slice(b * B, (b + 1) * B)
        total = own_ref[rows]
        for ref, step in zip((came_x, came_y), steps):
            total = total + from_code(ref[rows]) * step[b : b + 1]
        total = jnp.where(is_member(struct_ref, p, first + b), total, 0.0)
        high = total.astype(jnp.bfloat16)
        off_ref[rows] = high
        both[rows, :B] = high
        both[rows, B:] = (total - high.astype(jnp.float32)).astype(jnp.bfloat16)
    diag = jnp.dot(lower[...], both[...], preferred_element_type=jnp.float32)
    diag = diag[:, :B] + diag[:, B:]
    piece = B // 8
    for zz in range(4):
        for cc in range(2):
            flip = zz ^ z
            core = jnp.where(flip == 1, 0, jnp.where(flip == 2, 1, cc))
            slot = jnp.where(flip == 0, 3, jnp.where(flip == 3, 2, cc)) + 4 * (core ^ c)
            at = (2 * zz + cc) * piece
            diag_ref[pl.ds(pl.multiple_of(slot * piece, piece), piece)] = diag[at : at + piece]


def send(value, move):
    found = []
    for p in range(4):
        for z in range(4):
            for c in range(2):
                to = move(p, z, c)
                found.append((p * 8 + 2 * z + c, to[0] * 8 + 2 * to[1] + to[2]))
    return lax.ppermute(value, AXES, found)


def chip_swap(p, z, c):
    return (p, z, 1 - c)


def along(flip):
    return lambda p, z, c: (p, z ^ flip, c)


def across(flip):
    return lambda p, z, c: (p ^ flip, z, c)


def after(value, *earlier):
    return lax.optimization_barrier((value, *earlier))[0]


def line_body(ancestor_inverse, lower_panel, pivot_inverse, struct_list):
    rows, depth = ancestor_inverse.shape
    shard = lower_panel.shape[0]
    bf16, f32, i16 = jnp.bfloat16, jnp.float32, jnp.int16
    shape = jax.ShapeDtypeStruct
    piece = shape((shard, B), bf16)
    code, keep, to_x, to_y, to_both = call(
        code_kernel,
        (shape((shard, 3 * B), i16),) + (piece,) * 4,
        [VM],
        [],
        8 * shard * NK * B,
        4 * shard * NK * B,
        "code",
    )(lower_panel)
    def small(kernel, outs, name, *args, flops=1):
        return call(kernel, outs, [VM] * len(args), [], flops, 1, name, room=2**21)(*args)

    own_piece = keep
    far_one = send(keep, along(1))
    rows_x = send(to_x, across(1))
    rows_y = send(to_y, across(2))
    rows_both = send(to_both, across(3))
    gathered = lax.all_gather(code, "pcol", axis=0, tiled=True)

    coded = shape((rows + TAIL, B), i16)

    def sums(slots, outs, name, *args):
        return call(
            functools.partial(sums_kernel, slots),
            (coded,) * outs,
            [SM, VM, VM],
            [pltpu.VMEM((depth, outs * B), bf16)],
            1,
            1,
            name,
        )(*args)

    (part_d,) = sums(((0, 3),), 1, "sums_d", struct_list, ancestor_inverse, gathered)
    came_d = send(part_d, across(3))
    part_x, part_y = sums(
        ((1, 1), (2, 2)), 2, "sums_xy", after(struct_list, part_d), ancestor_inverse, gathered
    )
    came_x = send(part_x, across(1))
    stay, to_one, to_two, to_three = small(
        route_kernel, (piece,) * 4, "route", keep, rows_x, rows_y, rows_both, flops=8 * 10**9
    )
    to_one, to_two, to_three, _ = lax.optimization_barrier((to_one, to_two, to_three, part_d))
    from_one = send(to_one, along(1))
    trio = small(
        pair_kernel, shape((3 * shard, B), bf16), "pair", to_two, own_piece, far_one, flops=3 * 10**9
    )
    from_two = send(trio, along(2))
    pair, two = trio[shard:], from_two[shard:]
    their_pair = send(pair, chip_swap)
    def own_half(far, *args, flops=1):
        return call(
            functools.partial(own_kernel, far),
            shape((rows, B), f32),
            [SM] + [VM] * (1 + len(args)),
            [pltpu.VMEM((depth // 2, B), bf16)],
            flops,
            1,
            "own",
        )(struct_list, ancestor_inverse, *args)

    near_own = own_half(0, pair, their_pair)
    came_y = send(part_y, across(2))
    from_three = send(to_three, along(3))
    base = small(base_kernel, shape((rows, B), f32), "base", came_d, near_own, flops=4 * 10**9)
    own = own_half(1, two, send(two, chip_swap), base)
    half_rows = shape((2 * shard, B), bf16)
    keep, give = small(
        share_kernel, (half_rows, half_rows), "share", stay, from_one, from_two, from_three, flops=2 * 10**9
    )
    lower = call(
        turn_kernel,
        shape((B, rows), bf16),
        [VM, VM],
        [pltpu.VMEM((rows, B), bf16)],
        1,
        1,
        "turn",
    )(keep, send(give, chip_swap))
    off_inverse, diag = call(
        last_kernel,
        (shape((rows, B), bf16), shape((B, B), f32)),
        [SM] + [VM] * 4,
        [pltpu.VMEM((rows, 2 * B), bf16)],
        4 * rows * B * B,
        8 * rows * B,
        "last",
    )(struct_list, own, came_x, came_y, lower)

    half, part = B // 2, B // 8
    total = diag[:half] + send(diag[half:], chip_swap)
    pair = send(total[: 2 * part], lambda p, z, c: (p, z ^ (1 + c), c))
    total = total[3 * part :] + send(total[2 * part : 3 * part], along(3))
    even = lax.axis_index("pcol") % 2 == 0
    kept = jnp.where(even, pair[:part], pair[part:])
    other = send(jnp.where(even, pair[part:], pair[:part]), chip_swap)
    return off_inverse, pivot_inverse - (total + kept + other)


def body(ancestor_inverse, lower_panel, pivot_inverse, struct_list):
    rows, depth = ancestor_inverse.shape
    shard = lower_panel.shape[0]
    line = (
        lax.axis_size("prow") == 4
        and lax.axis_size("pcol") == 8
        and depth == 8 * shard
        and depth == 2 * rows
        and shard % 64 == 0
        and shard <= B
    )
    plan = line_body if line else general_body
    return plan(ancestor_inverse, lower_panel, pivot_inverse, struct_list)


def solution(mesh):
    placed = (P("pcol", "prow"), P(("prow", "pcol"), None), P("pcol", "prow"), P())
    return jax.shard_map(
        body,
        mesh=mesh,
        in_specs=placed,
        out_specs=(P("pcol", "prow"), P("pcol", "prow")),
        check_vma=False,
    )
```

```python
import functools

import jax
import jax.numpy as jnp
from jax import lax
from jax.experimental import pallas as pl
from jax.experimental.pallas import tpu as pltpu
from jax.sharding import PartitionSpec as P

B = 256
NK = 4
AXES = ("prow", "pcol")
TAIL = 16


def from_root(value, axis, root):
    mine = lax.axis_index(axis) == root
    return lax.psum(jnp.where(mine, value, jnp.zeros_like(value)), axis)


def membership(struct_list, ancestor_ids):
    listed = struct_list[:, :, None] == ancestor_ids[None, None, :]
    return jnp.transpose(jnp.any(listed, axis=1))


def general_body(ancestor_inverse, lower_panel, pivot_inverse, struct_list):
    row_count = ancestor_inverse.shape[0] // B
    col_count = ancestor_inverse.shape[1] // B
    grid_rows = lax.axis_size("prow")
    prow_index = lax.axis_index("prow")
    pcol_index = lax.axis_index("pcol")
    col_share = NK * B // grid_rows
    gathered = lax.all_gather(lower_panel, "pcol", axis=0, tiled=True)
    col_ids = prow_index * col_count + jnp.arange(col_count, dtype=jnp.int32)
    row_ids = pcol_index * row_count + jnp.arange(row_count, dtype=jnp.int32)
    member_cols = membership(struct_list, col_ids)
    member_rows = membership(struct_list, row_ids)
    scaled = gathered.reshape(col_count, B, NK, B) * member_cols[:, None, :, None].astype(
        jnp.bfloat16
    )
    masked = scaled.reshape(col_count * B, NK * B)
    partial_value = -jnp.dot(ancestor_inverse, masked, preferred_element_type=jnp.float32)
    share_sum = lax.psum_scatter(partial_value, "prow", scatter_dimension=1, tiled=True)
    columns = prow_index * col_share + jnp.arange(col_share, dtype=jnp.int32)
    block_of = columns // B
    one_hot = block_of[:, None] == jnp.arange(NK, dtype=jnp.int32)[None, :]
    row_mask = jnp.any(member_rows[:, None, :] & one_hot[None, :, :], axis=2).astype(jnp.float32)
    off_share = (share_sum.reshape(row_count, B, col_share) * row_mask[:, None, :]).reshape(
        row_count * B, col_share
    )
    off_inverse = off_share.astype(jnp.bfloat16)
    block_count = max(col_share // B, 1)
    column_width = col_share // block_count
    offset_blocks = pcol_index * row_count % col_count
    root_row = pcol_index * row_count // col_count
    piece = lax.dynamic_slice_in_dim(masked, offset_blocks * B, row_count * B, 0)
    lower_rows = from_root(piece, "prow", root_row)
    first_block = prow_index * col_share // B
    lower_slice = lax.dynamic_slice_in_dim(lower_rows, first_block * B, block_count * B, 1)
    lower_blocks = lower_slice.astype(jnp.float32).reshape(row_count * B, block_count, B)
    off_blocks = off_share.reshape(row_count * B, block_count, column_width)
    diag_term = jnp.einsum(
        "ikr,ikc->rkc", lower_blocks, off_blocks, precision=lax.Precision.HIGHEST
    ).reshape(B, col_share)
    diag_share = lax.psum_scatter(diag_term, "pcol", scatter_dimension=0, tiled=True)
    diag_inverse = pivot_inverse - diag_share
    return (off_inverse, diag_inverse)


VM = pl.BlockSpec(memory_space=pltpu.VMEM)
SM = pl.BlockSpec(memory_space=pltpu.SMEM)
FINE = 64
TINY = 2.0**-100
FILL = 0.9999


def place():
    p = lax.axis_index("prow")
    q = lax.axis_index("pcol")
    return p, q // 2, q % 2


def call(kernel, outs, specs, scratch, flops, moved, name, room=2**23):
    return pl.pallas_call(
        kernel,
        out_shape=outs,
        in_specs=specs,
        out_specs=jax.tree.map(lambda _: VM, outs),
        scratch_shapes=scratch,
        compiler_params=pltpu.CompilerParams(vmem_limit_bytes=room),
        cost_estimate=pl.CostEstimate(flops=flops, bytes_accessed=moved, transcendentals=0),
        name=name,
    )


def is_member(struct_ref, level, ancestor):
    found = struct_ref[level, 0] == ancestor
    for slot in range(1, struct_ref.shape[1]):
        found = found | (struct_ref[level, slot] == ancestor)
    return found


def column_power(value):
    top = jnp.maximum(jnp.max(jnp.abs(value), axis=0, keepdims=True), 2e-34)
    power = jnp.floor(jnp.log2(top)) + 1.0
    return jnp.where(top >= jnp.exp2(power), power + 1.0, power)


def put_tail(ref, powers, rows):
    row = lax.broadcasted_iota(jnp.int32, (TAIL, ref.shape[1]), 0)
    tail = jnp.zeros((TAIL, ref.shape[1]), jnp.float32)
    for block, power in enumerate(powers):
        tail = jnp.where(row == block, power, tail)
    ref[rows : rows + TAIL] = tail.astype(jnp.int32).astype(jnp.int16)


def to_code(value):
    return jnp.round(value).astype(jnp.int32).astype(jnp.int16)


def from_code(code):
    return code.astype(jnp.int32).astype(jnp.float32)


def code_kernel(lower_ref, code_ref, own, to_x, to_y, to_both):
    p, _, _ = place()

    def level(k):
        return lower_ref[:, pl.ds(pl.multiple_of(k * B, B), B)]

    for flip, out in enumerate((own, to_x, to_y, to_both)):
        out[...] = level(p ^ flip)
    for slot, flip in enumerate((3, 1, 2)):
        value = level(p ^ flip).astype(jnp.float32)
        size = jnp.abs(value)
        power = jnp.floor(jnp.log2(jnp.maximum(size, TINY)))
        code = jnp.round(size * jnp.exp2(7.0 - power)) + (power + 126.0) * 128.0
        code = jnp.where(size < TINY, 0.0, jnp.where(value < 0.0, -code, code))
        code_ref[:, slot * B : (slot + 1) * B] = code.astype(jnp.int32).astype(jnp.int16)


def load_panel(code_ref, panel, struct_ref, slots):
    p, _, _ = place()
    blocks = panel.shape[0] // B
    for at, (slot, flip) in enumerate(slots):
        for block in range(blocks):
            rows = slice(block * B, (block + 1) * B)
            listed = is_member(struct_ref, p ^ flip, p * blocks + block)

            @pl.when(listed)
            def _(rows=rows, at=at, slot=slot):
                code = code_ref[rows, slot * B : (slot + 1) * B].astype(jnp.int32)
                size = jnp.abs(code)
                power = jnp.exp2(((size >> 7) - 134).astype(jnp.float32))
                value = ((size & 127) + 128).astype(jnp.float32) * power
                panel[rows, at * B : (at + 1) * B] = jnp.where(code < 0, -value, value).astype(
                    jnp.bfloat16
                )

            @pl.when(jnp.logical_not(listed))
            def _(rows=rows, at=at):
                panel[rows, at * B : (at + 1) * B] = jnp.zeros((B, B), jnp.bfloat16)


def sums_kernel(slots, struct_ref, a_ref, code_ref, *refs):
    outs, panel = refs[:-1], refs[-1]
    load_panel(code_ref, panel, struct_ref, slots)
    blocks = a_ref.shape[0] // B
    powers = [[] for _ in outs]
    for b in range(blocks):
        rows = slice(b * B, (b + 1) * B)
        total = -jnp.dot(a_ref[rows], panel[...], preferred_element_type=jnp.float32)
        for i, ref in enumerate(outs):
            part = total[:, i * B : (i + 1) * B]
            power = column_power(part)
            ref[rows] = to_code(part * (jnp.exp2(15.0 - power) * FILL))
            powers[i].append(power)
    for ref, power in zip(outs, powers):
        put_tail(ref, power, blocks * B)


def came_step(ref, blocks):
    return jnp.exp2(from_code(ref[blocks * B : blocks * B + TAIL]) - 15.0) * (1.0 / FILL)


def pair_kernel(to_two, own_ref, one_ref, out_ref):
    shard = own_ref.shape[0]
    for at, ref in enumerate((to_two, own_ref, one_ref)):
        out_ref[at * shard : (at + 1) * shard] = ref[...]


def base_kernel(came_ref, near_ref, base_ref):
    blocks = base_ref.shape[0] // B
    step = came_step(came_ref, blocks)
    for b in range(blocks):
        rows = slice(b * B, (b + 1) * B)
        base_ref[rows] = near_ref[rows] + from_code(came_ref[rows]) * step[b : b + 1]


def own_kernel(far, struct_ref, a_ref, mine, theirs, *refs):
    own_ref, panel = refs[-2:]
    p, z, c = place()
    shard = mine.shape[0] // 2
    half = (z // 2) ^ far
    for i in range(2):
        chip = ((z ^ i) % 2) * 2
        for ref, core in ((mine, c), (theirs, 1 - c)):
            at = pl.multiple_of((chip + core) * shard, FINE)
            panel[pl.ds(at, shard)] = ref[i * shard : (i + 1) * shard]
    blocks = panel.shape[0] // B
    for block in range(blocks):
        listed = is_member(struct_ref, p, (2 * p + half) * blocks + block)

        @pl.when(jnp.logical_not(listed))
        def _(block=block):
            panel[block * B : (block + 1) * B] = jnp.zeros((B, B), jnp.bfloat16)

    depth = panel.shape[0]
    columns = a_ref[:, pl.ds(pl.multiple_of(half * depth, depth), depth)]
    total = -jnp.dot(columns, panel[...], preferred_element_type=jnp.float32)
    own_ref[...] = total + refs[0][...] if far else total


def route_kernel(own, x, y, both, *outs):
    p, z, _ = place()
    for flip, out in enumerate(outs):
        for turn, ref in enumerate((own, x, y, both)):

            @pl.when((p ^ z) == (turn ^ flip))
            def _(ref=ref, out=out):
                out[...] = ref[...]


def share_kernel(own, one, two, three, keep_ref, give_ref):
    _, z, c = place()
    shard = own.shape[0]
    for flip, ref in enumerate((own, one, two, three)):
        chip = z ^ flip
        at = pl.multiple_of((chip % 2) * shard, 64)

        @pl.when(chip // 2 == c)
        def _(ref=ref, at=at):
            keep_ref[pl.ds(at, shard)] = ref[:shard]

        @pl.when(chip // 2 != c)
        def _(ref=ref, at=at):
            give_ref[pl.ds(at, shard)] = ref[:shard]


def turn_kernel(keep, came, out_ref, lower):
    _, _, c = place()
    shard = keep.shape[0] // 2
    for half in range(2):
        for ref, core in ((keep, c), (came, 1 - c)):
            at = pl.multiple_of((2 * half + core) * shard, FINE)
            lower[pl.ds(at, shard)] = ref[half * shard : (half + 1) * shard]
    out_ref[...] = jnp.transpose(lower[...])


def last_kernel(
    struct_ref, own_ref, came_x, came_y, lower, off_ref, diag_ref, both
):
    p, z, c = place()
    blocks = off_ref.shape[0] // B
    first = (2 * z + c) * blocks
    steps = [came_step(ref, blocks) for ref in (came_x, came_y)]
    for b in range(blocks):
        rows = slice(b * B, (b + 1) * B)
        total = own_ref[rows]
        for ref, step in zip((came_x, came_y), steps):
            total = total + from_code(ref[rows]) * step[b : b + 1]
        total = jnp.where(is_member(struct_ref, p, first + b), total, 0.0)
        high = total.astype(jnp.bfloat16)
        off_ref[rows] = high
        both[rows, :B] = high
        both[rows, B:] = (total - high.astype(jnp.float32)).astype(jnp.bfloat16)
    diag = jnp.dot(lower[...], both[...], preferred_element_type=jnp.float32)
    diag = diag[:, :B] + diag[:, B:]
    piece = B // 8
    for zz in range(4):
        for cc in range(2):
            flip = zz ^ z
            core = jnp.where(flip == 1, 0, jnp.where(flip == 2, 1, cc))
            slot = jnp.where(flip == 0, 3, jnp.where(flip == 3, 2, cc)) + 4 * (core ^ c)
            at = (2 * zz + cc) * piece
            diag_ref[pl.ds(pl.multiple_of(slot * piece, piece), piece)] = diag[at : at + piece]


def send(value, move):
    found = []
    for p in range(4):
        for z in range(4):
            for c in range(2):
                to = move(p, z, c)
                found.append((p * 8 + 2 * z + c, to[0] * 8 + 2 * to[1] + to[2]))
    return lax.ppermute(value, AXES, found)


def chip_swap(p, z, c):
    return (p, z, 1 - c)


def along(flip):
    return lambda p, z, c: (p, z ^ flip, c)


def across(flip):
    return lambda p, z, c: (p ^ flip, z, c)


def after(value, *earlier):
    return lax.optimization_barrier((value, *earlier))[0]


def line_body(ancestor_inverse, lower_panel, pivot_inverse, struct_list):
    rows, depth = ancestor_inverse.shape
    shard = lower_panel.shape[0]
    bf16, f32, i16 = jnp.bfloat16, jnp.float32, jnp.int16
    shape = jax.ShapeDtypeStruct
    piece = shape((shard, B), bf16)
    code, keep, to_x, to_y, to_both = call(
        code_kernel,
        (shape((shard, 3 * B), i16),) + (piece,) * 4,
        [VM],
        [],
        8 * shard * NK * B,
        4 * shard * NK * B,
        "code",
    )(lower_panel)
    def small(kernel, outs, name, *args, flops=1):
        return call(kernel, outs, [VM] * len(args), [], flops, 1, name, room=2**21)(*args)

    own_piece = keep
    far_one = send(keep, along(1))
    rows_x = send(to_x, across(1))
    rows_y = send(to_y, across(2))
    rows_both = send(to_both, across(3))
    gathered = lax.all_gather(code, "pcol", axis=0, tiled=True)

    coded = shape((rows + TAIL, B), i16)

    def sums(slots, outs, name, *args):
        return call(
            functools.partial(sums_kernel, slots),
            (coded,) * outs,
            [SM, VM, VM],
            [pltpu.VMEM((depth, outs * B), bf16)],
            1,
            1,
            name,
        )(*args)

    (part_d,) = sums(((0, 3),), 1, "sums_d", struct_list, ancestor_inverse, gathered)
    came_d = send(part_d, across(3))
    part_x, part_y = sums(
        ((1, 1), (2, 2)), 2, "sums_xy", after(struct_list, part_d), ancestor_inverse, gathered
    )
    came_x = send(part_x, across(1))
    stay, to_one, to_two, to_three = small(
        route_kernel, (piece,) * 4, "route", keep, rows_x, rows_y, rows_both, flops=10**10
    )
    to_one, to_two, to_three, _ = lax.optimization_barrier((to_one, to_two, to_three, part_d))
    from_one = send(to_one, along(1))
    trio = small(
        pair_kernel, shape((3 * shard, B), bf16), "pair", to_two, own_piece, far_one, flops=3 * 10**9
    )
    from_two = send(trio, along(2))
    pair, two = trio[shard:], from_two[shard:]
    their_pair = send(pair, chip_swap)
    def own_half(far, *args, flops=1):
        return call(
            functools.partial(own_kernel, far),
            shape((rows, B), f32),
            [SM] + [VM] * (1 + len(args)),
            [pltpu.VMEM((depth // 2, B), bf16)],
            flops,
            1,
            "own",
        )(struct_list, ancestor_inverse, *args)

    near_own = own_half(0, pair, their_pair)
    came_y = send(after(part_y, near_own), across(2))
    from_three = send(to_three, along(3))
    base = small(base_kernel, shape((rows, B), f32), "base", came_d, near_own, flops=6 * 10**9)
    own = own_half(1, two, send(two, chip_swap), base)
    half_rows = shape((2 * shard, B), bf16)
    keep, give = small(
        share_kernel, (half_rows, half_rows), "share", stay, from_one, from_two, from_three, flops=2 * 10**9
    )
    lower = call(
        turn_kernel,
        shape((B, rows), bf16),
        [VM, VM],
        [pltpu.VMEM((rows, B), bf16)],
        1,
        1,
        "turn",
    )(keep, send(give, chip_swap))
    off_inverse, diag = call(
        last_kernel,
        (shape((rows, B), bf16), shape((B, B), f32)),
        [SM] + [VM] * 4,
        [pltpu.VMEM((rows, 2 * B), bf16)],
        4 * rows * B * B,
        8 * rows * B,
        "last",
    )(struct_list, own, came_x, came_y, lower)

    half, part = B // 2, B // 8
    total = diag[:half] + send(diag[half:], chip_swap)
    pair = send(total[: 2 * part], lambda p, z, c: (p, z ^ (1 + c), c))
    total = total[3 * part :] + send(total[2 * part : 3 * part], along(3))
    even = lax.axis_index("pcol") % 2 == 0
    kept = jnp.where(even, pair[:part], pair[part:])
    other = send(jnp.where(even, pair[part:], pair[:part]), chip_swap)
    return off_inverse, pivot_inverse - (total + kept + other)


def body(ancestor_inverse, lower_panel, pivot_inverse, struct_list):
    rows, depth = ancestor_inverse.shape
    shard = lower_panel.shape[0]
    line = (
        lax.axis_size("prow") == 4
        and lax.axis_size("pcol") == 8
        and depth == 8 * shard
        and depth == 2 * rows
        and shard % 64 == 0
        and shard <= B
    )
    plan = line_body if line else general_body
    return plan(ancestor_inverse, lower_panel, pivot_inverse, struct_list)


def solution(mesh):
    placed = (P("pcol", "prow"), P(("prow", "pcol"), None), P("pcol", "prow"), P())
    return jax.shard_map(
        body,
        mesh=mesh,
        in_specs=placed,
        out_specs=(P("pcol", "prow"), P("pcol", "prow")),
        check_vma=False,
    )
```
